128 devices in a mesh: dp: 8 (over x_hi, y), tensor: 16 (over z, x_lo, core).
Axes of the slice: x: 4 (x_hi: 2, x_lo: 2; x = x_hi * 2 + x_lo), y: 4, z: 4, core: 2. Of those that a mesh axis runs over, the one named last changes fastest.
Arguments:
- inputs: bfloat16 [1024, 6144], P('dp'), may hold values from -6 to 6
- targets: bfloat16 [1024, 6144], P('dp'), may hold values from -6 to 6
- lengths: int32 [8], P('dp'), may hold values from 1 to 128, 768 in all
- ln_gain: float32 [6144], replicated, may hold values from 0.5 to 1.5
- ln_bias: float32 [6144], replicated, may hold values from -0.8 to 0.8
- query_weight: bfloat16 [6144, 6144], P(None, 'tensor'), may hold values from -0.078125 to 0.078125
- w_key: bfloat16 [6144, 6144], P(None, 'tensor'), may hold values from -0.078125 to 0.078125
- value_weight: bfloat16 [6144, 6144], P(None, 'tensor'), may hold values from -0.078125 to 0.078125
- w_out: bfloat16 [6144, 6144], P('tensor'), may hold values from -0.078125 to 0.078125
- down_query: bfloat16 [6144, 16], replicated, may hold values from -0.078125 to 0.078125
- down_value: bfloat16 [6144, 16], replicated, may hold values from -0.078125 to 0.078125
- query_up_factor: float32 [16, 6144], P(None, 'tensor'), may hold values from -0.6 to 0.6
- value_up_factor: float32 [16, 6144], P(None, 'tensor'), may hold values from -0.6 to 0.6
Outputs:
- step_query: float32 [16, 6144], P(None, 'tensor')
- step_value: float32 [16, 6144], P(None, 'tensor')
- remain_query: float32 [16, 6144], P(None, 'tensor')
- remain_value: float32 [16, 6144], P(None, 'tensor')
The draws below stay inside these ranges and needn't reach their ends.
Inputs may be any that keep to these rules, and one draw needn't show every extreme that they name: `lengths`: live tokens of each sequence; one sequence has exactly 128.
All inputs are finite; a program needn't handle non-finite values. No bound on the sum of `lengths` on one device may be relied on, other than what follows from the above.
Results may differ from the reference program's by a relative error of at most 0.035.
Values sent between devices are 32-bit elements; how exact they have to be, the bound alone decides.
A program may use at most 128 MiB of HBM per device.

```python
import math
import jax
import jax.numpy as jnp
import numpy as np
from jax import lax

D = 6144
HEAD_DIM = 128
R = 16
LENGTH = 128
CG_STEPS = 3
INNER = 6144
SEQS = 8
TOKENS = 1024
N_DP = 8


def block_scale(own_key, extent, cuts, least, top_value):
    loudness = 1.0
    for dim, blocks in cuts:
        draws = jax.random.uniform(jax.random.fold_in(jax.random.fold_in(own_key, 6), dim), (blocks,), jnp.float32, least / len(cuts), top_value / len(cuts))
        loudness = loudness * jnp.repeat(jnp.exp(draws), extent[dim] // blocks).reshape((-1,) + (1,) * (len(extent) - 1 - dim))
    return loudness


def length_profile(number_of, total, reach, slope):
    weights = [(1 << 20) // math.isqrt(grade ** slope) + 1 for grade in range(2, number_of + 1)]
    rest, given = total - reach - (number_of - 1), [1] * (number_of - 1)
    while rest > 0:
        free = [i for i in range(number_of - 1) if given[i] < reach]
        pool, remaining = sum([weights[i] for i in free]), rest
        for i in free:
            more = min(reach - given[i], max(1, remaining * weights[i] // pool), rest)
            given[i] = given[i] + more
            rest = rest - more
    return np.array([reach] + given)


def ragged(rng, amount, total, bound, lean):
    if amount == 2:
        one = jax.random.randint(rng, (), max(1, total - bound), min(bound, total - 1) + 1)
        return jnp.stack([one, total - one])
    sizes = jnp.asarray(length_profile(amount, total, bound, lean), jnp.int32)
    pairs = (amount - 1) // 2
    source_of, receiver = sizes[1:1 + 2 * pairs:2], sizes[2:2 + 2 * pairs:2]
    room = jnp.minimum(source_of - 1, bound - receiver)
    shifted = jax.random.randint(jax.random.fold_in(rng, 1), (pairs,), 0, 1 << 20) % (room + 1)
    sizes = sizes.at[1:1 + 2 * pairs:2].set(source_of - shifted).at[2:2 + 2 * pairs:2].set(receiver + shifted)
    return sizes[jax.random.permutation(jax.random.fold_in(rng, 2), amount)]


def scatter_about(key, extent, width, most, pieces=(), kind=jnp.bfloat16):
    entries = jax.random.normal(key, extent, jnp.float32) * width
    if len(pieces) > 0:
        entries = block_scale(key, extent, pieces, -0.22, 0.18) * entries
    return jnp.clip(entries, min=-most, max=most).astype(kind)


def setup_inputs(seed: int = 0) -> dict:
    arg_keys = jax.random.split(jax.random.key(seed), 14)
    inputs = scatter_about(arg_keys[0], (TOKENS, D), 1.0, 6.0, ((0, 8),))
    targets = scatter_about(arg_keys[1], (TOKENS, D), 1.0, 6.0, ((0, 8),))
    lengths = ragged(arg_keys[2], SEQS, N_DP * LENGTH * 3 // 4, LENGTH, 1).astype(jnp.int32)
    ln_gain = jnp.clip(1.0 + 0.1 * jax.random.normal(arg_keys[3], (D,), jnp.float32), 0.5, 1.5)
    ln_bias = scatter_about(arg_keys[4], (D,), 0.2, 0.8, (), jnp.float32)
    query_weight = scatter_about(arg_keys[5], (D, INNER), D ** -0.5, 0.078125, ((1, 16),))
    w_key = scatter_about(arg_keys[6], (D, INNER), D ** -0.5, 0.078125, ((1, 16),))
    value_weight = scatter_about(arg_keys[7], (D, INNER), D ** -0.5, 0.078125, ((1, 16),))
    w_out = scatter_about(arg_keys[8], (INNER, D), INNER ** -0.5, 0.078125, ((0, 16),))
    down_query = scatter_about(arg_keys[9], (D, R), D ** -0.5, 0.078125)
    down_value = scatter_about(arg_keys[10], (D, R), D ** -0.5, 0.078125)
    query_up_factor = scatter_about(arg_keys[11], (R, INNER), 0.1, 0.6, ((1, 16),), jnp.float32)
    value_up_factor = scatter_about(arg_keys[12], (R, INNER), 0.1, 0.6, ((1, 16),), jnp.float32)
    return dict(inputs=inputs, targets=targets, lengths=lengths, ln_gain=ln_gain, ln_bias=ln_bias, query_weight=query_weight, w_key=w_key, value_weight=value_weight, w_out=w_out, down_query=down_query, down_value=down_value, query_up_factor=query_up_factor, value_up_factor=value_up_factor)


EPS = 1e-05
ADAPTER_SCALE = 2.0
DAMP = 0.05
NEG = -1e+30

def layer_norm(rows, gain, bias):
    rows = rows.astype(jnp.float32)
    centred = rows - lax.optimization_barrier(jnp.mean(rows, axis=-1, keepdims=True))
    spread = lax.optimization_barrier(jnp.mean(centred * centred, axis=-1, keepdims=True))
    return (centred * lax.rsqrt(spread + EPS) * gain + bias).astype(jnp.bfloat16)

def attend(ups, normalized_input, query_weight, w_key, value_weight, w_out, down_query, down_value, live):
    query_up_factor, value_up_factor = ups
    length = normalized_input.shape[0]
    heads = query_weight.shape[1] // HEAD_DIM
    query_down_factor = jnp.dot(normalized_input, down_query, preferred_element_type=jnp.float32)
    value_down_factor = jnp.dot(normalized_input, down_value, preferred_element_type=jnp.float32)
    query_rows = jnp.dot(normalized_input, query_weight, preferred_element_type=jnp.float32) + ADAPTER_SCALE * jnp.dot(query_down_factor, query_up_factor, precision=lax.Precision.HIGHEST)
    value_rows = jnp.dot(normalized_input, value_weight, preferred_element_type=jnp.float32) + ADAPTER_SCALE * jnp.dot(value_down_factor, value_up_factor, precision=lax.Precision.HIGHEST)
    keys = jnp.dot(normalized_input, w_key, preferred_element_type=jnp.float32)
    query_rows = query_rows.astype(jnp.bfloat16).reshape(length, heads, HEAD_DIM)
    value_rows = value_rows.astype(jnp.bfloat16).reshape(length, heads, HEAD_DIM)
    keys = keys.astype(jnp.bfloat16).reshape(length, heads, HEAD_DIM)
    scores = jnp.einsum('qhd,khd->hqk', query_rows.astype(jnp.float32), keys.astype(jnp.float32)) * HEAD_DIM ** (-0.5)
    scores = jnp.where(live[None], scores, NEG)
    top = lax.stop_gradient(lax.optimization_barrier(jnp.max(scores, axis=-1, keepdims=True)))
    weights = jnp.exp(scores - top)
    probs = (weights / lax.optimization_barrier(jnp.sum(weights, axis=-1, keepdims=True))).astype(jnp.bfloat16)
    mixed = jnp.einsum('hqk,khd->qhd', probs.astype(jnp.float32), value_rows.astype(jnp.float32))
    mixed = mixed.astype(jnp.bfloat16).reshape(length, heads * HEAD_DIM)
    return jnp.dot(mixed, w_out, preferred_element_type=jnp.float32)

def linear_parts(apply, ups):
    output, pullback = jax.vjp(apply, ups)

    def backward(cotan):
        return pullback(cotan)[0]

    def forward(vector):
        _, undo = jax.vjp(backward, jnp.zeros_like(output))
        return undo(vector)[0]
    return (output, forward, backward)

def local_dot(first, second):
    return jnp.sum(first[0] * second[0]) + jnp.sum(first[1] * second[1])

def reference(inputs, targets, lengths, ln_gain, ln_bias, query_weight, w_key, value_weight, w_out, down_query, down_value, query_up_factor, value_up_factor):
    places = jnp.arange(LENGTH, dtype=jnp.int32)
    seq_inputs = inputs.reshape(SEQS, LENGTH, D)
    seq_targets = targets.reshape(SEQS, LENGTH, D)
    ups = (query_up_factor, value_up_factor)
    zeros = (jnp.zeros_like(query_up_factor), jnp.zeros_like(value_up_factor))

    def linear_map(x_seq, len_seq):
        normalized_input = layer_norm(x_seq, ln_gain, ln_bias)
        live = (places[None, :] <= places[:, None]) & (places[None, :] < len_seq)
        row_live = (places < len_seq).astype(jnp.float32)

        def apply(weights):
            return attend(weights, normalized_input, query_weight, w_key, value_weight, w_out, down_query, down_value, live)
        output, forward, backward = linear_parts(apply, ups)
        return (output, forward, backward, row_live)

    def grad_step(total, item):
        x_seq, t_seq, len_seq = item
        output, forward, backward, row_live = linear_map(x_seq, len_seq)
        gap = x_seq.astype(jnp.float32) - t_seq.astype(jnp.float32)
        error = row_live[:, None] * (output + gap)
        back = backward(error / TOKENS)
        return ((total[0] + back[0], total[1] + back[1]), None)
    grads, _ = lax.scan(grad_step, zeros, (seq_inputs, seq_targets, lengths))

    def product(vector):

        def step(total, item):
            x_seq, len_seq = item
            output, forward, backward, row_live = linear_map(x_seq, len_seq)
            tangent = row_live[:, None] * forward(vector)
            back = backward(tangent / TOKENS)
            return ((total[0] + back[0], total[1] + back[1]), None)
        summed, _ = lax.scan(step, zeros, (seq_inputs, lengths))
        return (summed[0] + DAMP * vector[0], summed[1] + DAMP * vector[1])
    newton = zeros
    remain = (-grads[0], -grads[1])
    direction = remain
    norm_now = local_dot(remain, remain)
    for index in range(CG_STEPS):
        image = product(direction)
        alpha = norm_now / local_dot(direction, image)
        newton = (newton[0] + alpha * direction[0], newton[1] + alpha * direction[1])
        remain = (remain[0] - alpha * image[0], remain[1] - alpha * image[1])
        norm_next = local_dot(remain, remain)
        ratio = norm_next / norm_now
        direction = (remain[0] + ratio * direction[0], remain[1] + ratio * direction[1])
        norm_now = norm_next
    return (newton[0], newton[1], remain[0], remain[1])
```

```python
import jax
import jax.numpy as jnp
from jax import lax
from jax.experimental import pallas as pl
from jax.experimental.pallas import tpu as pltpu
from jax.sharding import PartitionSpec as P

HEAD_DIM = 128
CG_STEPS = 3
HEADS = 3
COLS = HEADS * HEAD_DIM
ROWS = 128
HALF = ROWS // 2
RANK = 16
WIDTH = 6144
CORE_WIDTH = WIDTH // 2
CHUNKS = CORE_WIDTH // COLS
N_DP = 8
N_Z = 4

EPS = 1e-05
ADAPTER_SCALE = 2.0
DAMP = 0.05
NEG = -1e30

F32 = jnp.float32
BF16 = jnp.bfloat16
MESH = pl.DeviceIdType.MESH

S_W, S_E1, S_S1, S_X1, S_S2, S_Z1, S_X2, S_S3, S_Z2 = 0, 8, 9, 10, 14, 15, 18, 21, 24
S_G, S_S4, S_S5, S_S6, S_E2, S_AR, N_SEND = 25, 39, 42, 43, 44, 45, 52
R_W, R_E1, R_S1, R_X1, R_S2, R_Z1, R_X2, R_S3, R_Z2 = 0, 8, 9, 10, 14, 15, 18, 21, 25
R_G, R_S4, R_S5, R_S6, R_E2, R_AR, N_RECV = 26, 42, 46, 47, 48, 49, 65


def dot(a, b):
    return lax.dot_general(a, b, (((1,), (0,)), ((), ())), preferred_element_type=F32)


def dot_t(a, b):
    return lax.dot_general(a, b, (((1,), (1,)), ((), ())), preferred_element_type=F32)


def split_high_low(x):
    high = x.astype(BF16)
    return high, (x - high.astype(F32)).astype(BF16)


def total(x):
    return jnp.sum(jnp.sum(x, axis=1, keepdims=True), axis=0, keepdims=True)


def kernel(
    len_ref,
    q_ref,
    k_ref,
    v_ref,
    uq_ref,
    uv_ref,
    uqt_ref,
    uvt_ref,
    gap_ref,
    w_ref,
    step_ref,
    remain_ref,
    wb,
    wtmp,
    wsend,
    wrecv,
    pf,
    pb,
    pbt,
    u3,
    ut,
    dmcat,
    e1s,
    e1r,
    part,
    rx1,
    rz1,
    rx2,
    rz2,
    gat,
    cprev,
    cot,
    e2r,
    arb,
    state,
    sca,
    s1r,
    s2r,
    s3b,
    s4b,
    s5r,
    s6r,
    lsem,
    ssem,
    rsem,
):
    d = lax.axis_index("dp")
    t = lax.axis_index("tensor")
    c = lax.rem(t, 2)
    x = lax.rem(t // 2, 2)
    z = t // 4
    sib = (d, t + 1 - 2 * c)
    xn = (d, t + 2 - 4 * x)

    def zn(off):
        return (d, lax.rem(t + 4 * off, 16))

    def dpn(off):
        return (lax.rem(d + off, N_DP), t)

    def remote(src, dst, s, r, device):
        return pltpu.make_async_remote_copy(
            src_ref=src,
            dst_ref=dst,
            send_sem=ssem.at[s],
            recv_sem=rsem.at[r],
            device_id=device,
            device_id_type=MESH,
        )

    barrier = pltpu.get_barrier_semaphore()
    partners = [sib, xn] + [zn(o) for o in (1, 2, 3)] + [dpn(o) for o in range(1, 8)]
    for device in partners:
        pl.semaphore_signal(barrier, inc=1, device_id=device, device_id_type=MESH)

    def own_copy(j):
        columns = pl.ds(pl.multiple_of(c * CORE_WIDTH + j * COLS, COLS), COLS)
        return pltpu.make_async_copy(
            w_ref.at[:, columns], wb.at[j, pl.ds(0, COLS)], lsem.at[j]
        )

    def other_copy(j):
        columns = pl.ds(pl.multiple_of((1 - c) * CORE_WIDTH + j * COLS, COLS), COLS)
        return pltpu.make_async_copy(w_ref.at[:, columns], wtmp.at[j], lsem.at[CHUNKS + j])

    def w_copy(j):
        return remote(wsend.at[j], wrecv.at[j], S_W + j, R_W + j, sib)

    @pl.loop(0, CHUNKS)
    def _(j):
        other_copy(j).start()

    @pl.loop(0, CHUNKS)
    def _(j):
        own_copy(j).start()

    pl.semaphore_wait(barrier, len(partners))

    @pl.loop(0, CHUNKS)
    def _(j):
        other_copy(j).wait()
        wsend[j] = wtmp[j].astype(F32)
        w_copy(j).start()

    limit = len_ref[0]
    row = lax.broadcasted_iota(jnp.int32, (ROWS, ROWS), 0)
    col = lax.broadcasted_iota(jnp.int32, (ROWS, ROWS), 1)
    live = (col <= row) & (col < limit)
    for h in range(HEADS):
        lanes = pl.ds(h * HEAD_DIM, HEAD_DIM)
        scores = dot_t(q_ref[:, lanes], k_ref[:, lanes]) * HEAD_DIM ** (-0.5)
        scores = jnp.where(live, scores, NEG)
        weights = jnp.exp(scores - jnp.max(scores, axis=-1, keepdims=True))
        probs = weights / jnp.sum(weights, axis=-1, keepdims=True)
        pf[h] = probs
        pb[h] = probs.astype(BF16)
        pbt[h] = probs.T.astype(BF16)
        mixed = dot(probs.astype(BF16), v_ref[:, lanes]).astype(BF16)
        dmcat[:, lanes] = mixed
        e1s[h] = mixed.astype(F32)
    for i, ref in enumerate((uq_ref, uv_ref)):
        high, low = split_high_low(ref[...])
        u3[i] = jnp.concatenate([high, high, low], axis=1)
    for i, ref in enumerate((uqt_ref, uvt_ref)):
        high, low = split_high_low(ref[...])
        ut[i] = jnp.concatenate([high, low], axis=0)
    own_rows = lax.broadcasted_iota(jnp.int32, (HALF, COLS), 0) + x * HALF
    mask = (own_rows < limit).astype(F32)
    cprev[0] = gap_ref[0] * mask
    cprev[1] = gap_ref[1] * mask
    state[...] = jnp.zeros_like(state)
    sca[...] = jnp.zeros_like(sca)

    @pl.loop(0, CHUNKS)
    def _(j):
        own_copy(j).wait()
        w_copy(j).wait_recv()
        wb[j, pl.ds(COLS, COLS)] = wrecv[j].astype(BF16)
        w_copy(j).wait_send()

    @pl.loop(0, CG_STEPS + 1)
    def _(k):
        @pl.when(k > 0)
        def _():
            remain = state[0]
            tangents = []
            for i in range(2):
                high, low = split_high_low(remain[i * RANK : (i + 1) * RANK])
                stacked = jnp.concatenate([high, low, high], axis=0)
                tangents.append((ADAPTER_SCALE * dot(u3[i], stacked)).astype(BF16))
            dq, dv = tangents
            for h in range(HEADS):
                lanes = slice(h * HEAD_DIM, (h + 1) * HEAD_DIM)
                scores = dot_t(dq[:, lanes], k_ref[:, lanes]) * HEAD_DIM ** (-0.5)
                probs = pf[h]
                tilted = probs * scores
                dprobs = tilted - probs * jnp.sum(tilted, axis=-1, keepdims=True)
                left = jnp.concatenate([dprobs.astype(BF16), pb[h]], axis=1)
                right = jnp.concatenate([v_ref[:, lanes], dv[:, lanes]], axis=0)
                dmixed = dot(left, right).astype(BF16)
                dmcat[:, lanes] = dmixed
                e1s[h] = dmixed.astype(F32)

        e1 = remote(e1s, e1r, S_E1, R_E1, sib)
        e1.start()
        sca[4] = jnp.broadcast_to(total(state[0] * state[0]), (8, 128))
        s1 = remote(sca.at[4], s1r, S_S1, R_S1, sib)
        s1.start()
        e1.wait_recv()
        for h in range(HEADS):
            dmcat[:, pl.ds(COLS + h * HEAD_DIM, HEAD_DIM)] = e1r[h].astype(BF16)
        s1.wait_recv()
        sca[5] = sca[4] + s1r[...]
        s2 = remote(sca.at[5], s2r, S_S2, R_S2, xn)
        s2.start()

        def x1(zi):
            return remote(part.at[zi, 1 - x], rx1.at[zi], S_X1 + zi, R_X1 + zi, xn)

        def z1(off):
            there = N_Z + lax.rem(z + off, N_Z)
            return remote(part.at[there], rz1.at[off - 1], S_Z1 + off - 1, R_Z1 + off - 1, zn(off))

        @pl.loop(1, N_Z + 1)
        def _(off):
            zi = lax.rem(z + off, N_Z)
            for region in range(2):
                j = zi + region * N_Z
                product = dot(dmcat[...], wb[j])
                part[j, 0] = product[:HALF]
                part[j, 1] = product[HALF:]
                if region == 0:
                    x1(zi).start()
                else:

                    @pl.when(off < N_Z)
                    def _():
                        z1(off).start()

        s2.wait_recv()
        s3b[z] = sca[5] + s2r[...]

        def s3(off):
            return remote(s3b.at[z], s3b.at[z], S_S3 + off - 1, R_S3 + z, zn(off))

        def s3_in(off):
            zi = lax.rem(z + off, N_Z)
            return remote(s3b.at[zi], s3b.at[zi], S_S3 + off - 1, R_S3 + zi, zn(off))

        for off in (1, 2, 3):
            s3(off).start()

        def x2(off):
            there = lax.rem(z + off, N_Z)
            return remote(part.at[there, x], rx2.at[off - 1], S_X2 + off - 1, R_X2 + off - 1, zn(off))

        @pl.loop(1, N_Z + 1)
        def _(off):
            zi = lax.rem(z + off, N_Z)
            x1(zi).wait_recv()
            part[zi, x] = part[zi, x] + rx1[zi]

            @pl.when(off < N_Z)
            def _():
                x2(off).start()

        for off in (1, 2, 3):
            z1(off).wait_recv()
        part[N_Z + z] = part[N_Z + z] + rz1[0] + rz1[1] + rz1[2]
        z2 = remote(part.at[N_Z + z, 1 - x], rz2, S_Z2, R_Z2, xn)
        z2.start()

        for off in (1, 2, 3):
            s3_in(off).wait_recv()
        sca[0] = s3b[0] + s3b[1] + s3b[2] + s3b[3]
        ratio = sca[0] / jnp.where(k > 1, sca[1], 1.0)
        beta = jnp.where(k == 0, 1.0, jnp.where(k == 1, 0.0, ratio))
        beta_row = beta[0:1, 0:1]

        def g_out(half, j, s, device):
            return remote(gat.at[half, j], gat.at[half, j], S_G + s, R_G + half * CHUNKS + j, device)

        for off in (1, 2, 3):
            x2(off).wait_recv()
        cx = part[z, x] + rx2[0] + rx2[1] + rx2[2]
        cx = cx * mask + beta_row * cprev[0]
        cprev[0] = cx
        gat[x, z] = cx
        g_x = [g_out(x, z, off - 1, zn(off)) for off in (1, 2, 3)]
        g_x.append(g_out(x, z, 3, xn))
        for copy in g_x:
            copy.start()
        z2.wait_recv()
        cz = part[N_Z + z, x] + rz2[...]
        cz = cz * mask + beta_row * cprev[1]
        cprev[1] = cz
        gat[x, N_Z + z] = cz
        g_z = [g_out(x, N_Z + z, 7, xn)]
        g_z += [g_out(x, N_Z + z, 7 + off, zn(off)) for off in (1, 2, 3)]
        for copy in g_z:
            copy.start()

        direction = state[0] + beta_row * state[1]
        state[1] = direction
        s4b[z, 0] = jnp.broadcast_to(total(cx * cx) + total(cz * cz), (8, 128))
        s4b[z, 1] = jnp.broadcast_to(total(direction * direction), (8, 128))

        def s4(off):
            return remote(s4b.at[z], s4b.at[z], S_S4 + off - 1, R_S4 + z, zn(off))

        def s4_in(off):
            zi = lax.rem(z + off, N_Z)
            return remote(s4b.at[zi], s4b.at[zi], S_S4 + off - 1, R_S4 + zi, zn(off))

        for off in (1, 2, 3):
            s4(off).start()

        def accumulate(j, first=False):
            both = jnp.concatenate([gat[0, j], gat[1, j]], axis=0).astype(BF16)
            product = dot_t(both, wb[j])
            if first:
                cot[...] = product
            else:
                cot[...] = cot[...] + product

        g_out(1 - x, N_Z + z, 0, xn).wait_recv()
        g_zf = [g_out(1 - x, N_Z + z, 10 + off, zn(off)) for off in (1, 2, 3)]
        for copy in g_zf:
            copy.start()
        accumulate(N_Z + z, first=True)
        g_xf = []
        for off in (1, 3, 2):
            zi = lax.rem(z + off, N_Z)
            g_out(x, zi, 0, xn).wait_recv()
            g_xf.append(g_out(x, zi, 3 + off, xn))
            g_xf[-1].start()
        g_out(1 - x, z, 0, xn).wait_recv()
        accumulate(z)

        for off in (1, 2, 3):
            s4_in(off).wait_recv()
        sca[2] = s4b[0, 0] + s4b[1, 0] + s4b[2, 0] + s4b[3, 0]
        sca[3] = s4b[0, 1] + s4b[1, 1] + s4b[2, 1] + s4b[3, 1]
        s5 = remote(sca.at[pl.ds(2, 2)], s5r, S_S5, R_S5, xn)
        s5.start()

        @pl.loop(1, N_Z)
        def _(off):
            zi = lax.rem(z + off, N_Z)
            g_out(x, N_Z + zi, 0, zn(off)).wait_recv()
            g_out(1 - x, N_Z + zi, 0, zn(off)).wait_recv()
            accumulate(N_Z + zi)
            g_out(1 - x, zi, 0, xn).wait_recv()
            accumulate(zi)

        e2 = remote(cot.at[:, pl.ds(COLS, COLS)], e2r, S_E2, R_E2, sib)
        e2.start()
        s5.wait_recv()
        sca[6] = sca[2] + s5r[0]
        sca[7] = sca[3] + s5r[1]
        s6 = remote(sca.at[pl.ds(6, 2)], s6r, S_S6, R_S6, sib)
        s6.start()
        e2.wait_recv()
        s6.wait_recv()

        parity = lax.rem(k, 2)
        for h in range(HEADS):
            lanes = slice(h * HEAD_DIM, (h + 1) * HEAD_DIM)
            cotan = (cot[:, lanes] + e2r[:, lanes]).astype(BF16)
            dprobs = dot_t(cotan, v_ref[:, lanes])
            probs = pf[h]
            tilted = probs * dprobs
            dscores = tilted - probs * jnp.sum(tilted, axis=-1, keepdims=True)
            dscores = (dscores * HEAD_DIM ** (-0.5)).astype(BF16)
            dq = dot(dscores, k_ref[:, lanes]).astype(BF16)
            dv = dot(pbt[h], cotan).astype(BF16)
            for i, cotangent in enumerate((dq, dv)):
                both = dot(ut[i], cotangent)
                arb[parity, d, i * RANK : (i + 1) * RANK, lanes] = ADAPTER_SCALE * (
                    both[:RANK] + both[RANK:]
                )
        squares = sca[6] + s6r[0]
        for h in range(HEADS):
            arb[parity, d, 2 * RANK : 2 * RANK + 8, h * HEAD_DIM : (h + 1) * HEAD_DIM] = squares

        def ar(off):
            mine = arb.at[parity, d]
            return remote(mine, mine, S_AR + off - 1, R_AR + parity * N_DP + d, dpn(off))

        def ar_in(off):
            peer = lax.rem(d + off, N_DP)
            slot = arb.at[parity, peer]
            return remote(slot, slot, S_AR + off - 1, R_AR + parity * N_DP + peer, dpn(off))

        for off in range(1, N_DP):
            ar(off).start()

        e1.wait_send()
        s1.wait_send()
        s2.wait_send()
        for zi in range(N_Z):
            x1(zi).wait_send()
        for off in (1, 2, 3):
            z1(off).wait_send()
            x2(off).wait_send()
            s3(off).wait_send()
            s4(off).wait_send()
        z2.wait_send()
        for copy in g_x + g_z + g_zf + g_xf:
            copy.wait_send()
        s5.wait_send()
        e2.wait_send()
        s6.wait_send()

        for off in range(1, N_DP):
            ar_in(off).wait_recv()
        for off in range(1, N_DP):
            ar(off).wait_send()
        summed = arb[parity, 0]
        for peer in range(1, N_DP):
            summed = summed + arb[parity, peer]
        summed = summed * (1.0 / (ROWS * N_DP))
        image = summed[: 2 * RANK] + DAMP * state[1]
        squared = summed[2 * RANK :, :HEAD_DIM]
        curvature = squared + DAMP * (sca[7] + s6r[1])
        alpha = jnp.where(k == 0, 1.0, sca[0] / jnp.where(k == 0, 1.0, curvature))[0:1, 0:1]
        state[2] = state[2] + jnp.where(k == 0, 0.0, alpha) * state[1]
        state[0] = state[0] - alpha * image
        sca[1] = sca[0]

    step_ref[...] = state[2]
    remain_ref[...] = state[0]


def solve(lengths, q, k, v, uq, uv, gap, w_out):
    vmem = pl.BlockSpec(memory_space=pltpu.VMEM)
    square = (HEADS, HEAD_DIM, HEAD_DIM)
    block = (HALF, COLS)
    scratch = [
        pltpu.VMEM((CHUNKS, 2 * COLS, COLS), BF16),
        pltpu.VMEM((CHUNKS, COLS, COLS), BF16),
        pltpu.VMEM((CHUNKS, COLS, COLS), F32),
        pltpu.VMEM((CHUNKS, COLS, COLS), F32),
        pltpu.VMEM(square, F32),
        pltpu.VMEM(square, BF16),
        pltpu.VMEM(square, BF16),
        pltpu.VMEM((2, ROWS, 3 * RANK), BF16),
        pltpu.VMEM((2, 2 * RANK, ROWS), BF16),
        pltpu.VMEM((ROWS, 2 * COLS), BF16),
        pltpu.VMEM(square, F32),
        pltpu.VMEM(square, F32),
        pltpu.VMEM((CHUNKS, 2) + block, F32),
        pltpu.VMEM((N_Z,) + block, F32),
        pltpu.VMEM((N_Z - 1, 2) + block, F32),
        pltpu.VMEM((N_Z - 1,) + block, F32),
        pltpu.VMEM(block, F32),
        pltpu.VMEM((2, CHUNKS) + block, F32),
        pltpu.VMEM((2,) + block, F32),
        pltpu.VMEM((ROWS, 2 * COLS), F32),
        pltpu.VMEM((ROWS, COLS), F32),
        pltpu.VMEM((2, N_DP, 2 * RANK + 8, COLS), F32),
        pltpu.VMEM((3, 2 * RANK, COLS), F32),
        pltpu.VMEM((8, 8, 128), F32),
        pltpu.VMEM((8, 128), F32),
        pltpu.VMEM((8, 128), F32),
        pltpu.VMEM((N_Z, 8, 128), F32),
        pltpu.VMEM((N_Z, 2, 8, 128), F32),
        pltpu.VMEM((2, 8, 128), F32),
        pltpu.VMEM((2, 8, 128), F32),
        pltpu.SemaphoreType.DMA((2 * CHUNKS,)),
        pltpu.SemaphoreType.DMA((N_SEND,)),
        pltpu.SemaphoreType.DMA((N_RECV,)),
    ]
    shape = jax.ShapeDtypeStruct((2 * RANK, COLS), F32)
    return pl.pallas_call(
        kernel,
        out_shape=(shape, shape),
        in_specs=[pl.BlockSpec(memory_space=pltpu.SMEM)]
        + [vmem] * 8
        + [pl.BlockSpec(memory_space=pl.ANY)],
        out_specs=(vmem, vmem),
        scratch_shapes=scratch,
        compiler_params=pltpu.CompilerParams(
            collective_id=0, has_side_effects=True, vmem_limit_bytes=48 * 2**20
        ),
        cost_estimate=pl.CostEstimate(
            flops=8 * 2 * ROWS * WIDTH * COLS, bytes_accessed=8 * 2**20, transcendentals=0
        ),
        name="newton",
    )(lengths, q, k, v, uq, uv, uq.T, uv.T, gap, w_out)


def layer_norm(rows, gain, bias):
    rows = rows.astype(F32)
    centred = rows - jnp.mean(rows, axis=-1, keepdims=True)
    spread = jnp.mean(centred * centred, axis=-1, keepdims=True)
    return (centred * lax.rsqrt(spread + EPS) * gain + bias).astype(BF16)


def on_device(
    inputs,
    targets,
    lengths,
    ln_gain,
    ln_bias,
    query_weight,
    w_key,
    value_weight,
    w_out,
    down_query,
    down_value,
    query_up_factor,
    value_up_factor,
):
    normed = layer_norm(inputs, ln_gain, ln_bias)
    downs = jnp.concatenate([down_query, down_value], axis=1)
    both = jnp.dot(normed, downs, preferred_element_type=F32)
    uq, uv = both[:, :RANK], both[:, RANK:]

    def project(weight, low, up):
        rows = jnp.dot(normed, weight, preferred_element_type=F32)
        if up is not None:
            rows = rows + ADAPTER_SCALE * jnp.dot(low, up, precision=lax.Precision.HIGHEST)
        return rows.astype(BF16)

    q = project(query_weight, uq, query_up_factor)
    k = project(w_key, None, None)
    v = project(value_weight, uv, value_up_factor)

    t = lax.axis_index("tensor")
    top = (t // 2) % 2 * HALF
    gaps = []
    for region in range(2):
        left = t % 2 * CORE_WIDTH + region * (CORE_WIDTH // 2) + t // 4 * COLS
        parts = [lax.dynamic_slice(a, (top, left), (HALF, COLS)) for a in (inputs, targets)]
        gaps.append(parts[0].astype(F32) - parts[1].astype(F32))
    gap = jnp.stack(gaps)
    step, remain = solve(lengths, q, k, v, uq, uv, gap, w_out)
    return (step[:RANK], step[RANK:], remain[:RANK], remain[RANK:])


def solution(mesh):
    in_specs = (
        P("dp", None),
        P("dp", None),
        P("dp"),
        P(),
        P(),
        P(None, "tensor"),
        P(None, "tensor"),
        P(None, "tensor"),
        P("tensor", None),
        P(),
        P(),
        P(None, "tensor"),
        P(None, "tensor"),
    )
    out_specs = (P(None, "tensor"), P(None, "tensor"), P(None, "tensor"), P(None, "tensor"))
    return jax.shard_map(
        on_device, mesh=mesh, in_specs=in_specs, out_specs=out_specs, check_vma=False
    )
```

```python
import jax
import jax.numpy as jnp
from jax import lax
from jax.experimental import pallas as pl
from jax.experimental.pallas import tpu as pltpu
from jax.sharding import PartitionSpec as P

HEAD_DIM = 128
CG_STEPS = 3
HEADS = 3
COLS = HEADS * HEAD_DIM
ROWS = 128
HALF = ROWS // 2
RANK = 16
WIDTH = 6144
CORE_WIDTH = WIDTH // 2
STAGES = 3
LANES = 128
PAIR = 2 * LANES
CHUNKS = CORE_WIDTH // PAIR
N_DP = 8
N_Z = 4

EPS = 1e-05
ADAPTER_SCALE = 2.0
DAMP = 0.05
NEG = -1e30

F32 = jnp.float32
BF16 = jnp.bfloat16
MESH = pl.DeviceIdType.MESH

S_W, S_E1, S_S1, S_S2, S_S3, S_S6, S_E2, S_X1, S_Z1, S_X2 = 0, 12, 15, 16, 17, 20, 21, 22, 25, 34
S_Z2, S_X3, S_X4, S_Z4, S_AR, S_SQ, N_SEND = 43, 46, 55, 58, 67, 74, 81
R_W, R_E1, R_S1, R_S2, R_S3, R_S6, R_E2, R_X1, R_Z1, R_X2 = 0, 12, 15, 16, 17, 21, 22, 23, 26, 35
R_Z2, R_X3, R_X4, R_Z4, R_AR, R_SQ, N_RECV = 44, 47, 59, 62, 74, 90, 106

PEERS = ((1, 2), (1, 1), (1, 3), (0, 2), (1, 0), (0, 1), (0, 3))


def dot(a, b):
    return lax.dot_general(a, b, (((1,), (0,)), ((), ())), preferred_element_type=F32)


def dot_t(a, b):
    return lax.dot_general(a, b, (((1,), (1,)), ((), ())), preferred_element_type=F32)


def split_high_low(x):
    high = x.astype(BF16)
    return high, (x - high.astype(F32)).astype(BF16)


def total(x):
    return jnp.sum(jnp.sum(x, axis=1, keepdims=True), axis=0, keepdims=True)


def kernel(
    len_ref,
    q_ref,
    k_ref,
    v_ref,
    uq_ref,
    uv_ref,
    uqt_ref,
    uvt_ref,
    gap_x_ref,
    gap_z_ref,
    w_ref,
    step_ref,
    remain_ref,
    wb,
    wtmp,
    wsend,
    wrecv,
    pf,
    pb,
    pbt,
    u3,
    ut,
    dmcat,
    e1s,
    e1r,
    part_x,
    part_z,
    rx1,
    rz1,
    rx2,
    rz2,
    gx,
    gz,
    cprev_x,
    cprev_z,
    cot,
    e2r,
    arb,
    sqb,
    squares,
    state,
    sca,
    s1r,
    s2r,
    s3b,
    s6r,
    lsem,
    ssem,
    rsem,
):
    d = lax.axis_index("dp")
    t = lax.axis_index("tensor")
    c = lax.rem(t, 2)
    x = lax.rem(t // 2, 2)
    z = t // 4
    sib = (d, t + 1 - 2 * c)
    xn = (d, t + 2 - 4 * x)

    def zn(off):
        return (d, lax.rem(t + 4 * off, 16))

    def dpn(hop):
        return lax.rem(d // 4 + hop[0], 2) * 4 + lax.rem(d + hop[1], 4)

    def remote(src, dst, s, r, device):
        return pltpu.make_async_remote_copy(
            src_ref=src,
            dst_ref=dst,
            send_sem=ssem.at[s],
            recv_sem=rsem.at[r],
            device_id=device,
            device_id_type=MESH,
        )

    barrier = pltpu.get_barrier_semaphore()
    partners = [sib, xn] + [zn(o) for o in (1, 2, 3)] + [(dpn(hop), t) for hop in PEERS]
    for device in partners:
        pl.semaphore_signal(barrier, inc=1, device_id=device, device_id_type=MESH)

    def own_copy(j):
        columns = pl.ds(pl.multiple_of(c * CORE_WIDTH + j * PAIR, PAIR), PAIR)
        return pltpu.make_async_copy(
            w_ref.at[:, columns], wb.at[j, pl.ds(0, COLS)], lsem.at[j]
        )

    def other_copy(j):
        columns = pl.ds(pl.multiple_of((1 - c) * CORE_WIDTH + j * PAIR, PAIR), PAIR)
        return pltpu.make_async_copy(w_ref.at[:, columns], wtmp.at[j], lsem.at[CHUNKS + j])

    def w_copy(j):
        return remote(wsend.at[j], wrecv.at[j], S_W + j, R_W + j, sib)

    @pl.loop(0, CHUNKS)
    def _(j):
        other_copy(j).start()

    @pl.loop(0, CHUNKS)
    def _(j):
        own_copy(j).start()

    pl.semaphore_wait(barrier, len(partners))

    @pl.loop(0, CHUNKS)
    def _(j):
        other_copy(j).wait()
        wsend[j] = wtmp[j].astype(F32)
        w_copy(j).start()

    limit = len_ref[0]
    row = lax.broadcasted_iota(jnp.int32, (ROWS, ROWS), 0)
    col = lax.broadcasted_iota(jnp.int32, (ROWS, ROWS), 1)
    live = (col <= row) & (col < limit)
    for h in range(HEADS):
        lanes = pl.ds(h * HEAD_DIM, HEAD_DIM)
        scores = dot_t(q_ref[:, lanes], k_ref[:, lanes]) * HEAD_DIM ** (-0.5)
        scores = jnp.where(live, scores, NEG)
        weights = jnp.exp(scores - jnp.max(scores, axis=-1, keepdims=True))
        probs = weights / jnp.sum(weights, axis=-1, keepdims=True)
        pf[h] = probs
        pb[h] = probs.astype(BF16)
        pbt[h] = probs.T.astype(BF16)
        mixed = dot(probs.astype(BF16), v_ref[:, lanes]).astype(BF16)
        dmcat[:, lanes] = mixed
        e1s[h] = mixed.astype(F32)
    for i, ref in enumerate((uq_ref, uv_ref)):
        high, low = split_high_low(ref[...])
        u3[i] = jnp.concatenate([high, high, low], axis=1)
    for i, ref in enumerate((uqt_ref, uvt_ref)):
        high, low = split_high_low(ref[...])
        ut[i] = jnp.concatenate([high, low], axis=0)
    place = lax.broadcasted_iota(jnp.int32, (ROWS, LANES), 0)
    mask_z = (place < limit).astype(F32)
    mask_x = (place[:HALF] + x * HALF < limit).astype(F32)
    for s in range(STAGES):
        cprev_x[s] = gap_x_ref[s] * mask_x
        cprev_z[s] = gap_z_ref[s] * mask_z
    state[...] = jnp.zeros_like(state)
    sca[...] = jnp.zeros_like(sca)

    @pl.loop(0, CHUNKS)
    def _(j):
        own_copy(j).wait()
        w_copy(j).wait_recv()
        wb[j, pl.ds(COLS, COLS)] = wrecv[j].astype(BF16)
        w_copy(j).wait_send()

    @pl.loop(0, CG_STEPS + 1)
    def _(k):
        def e1(h):
            return remote(e1s.at[h], e1r.at[h], S_E1 + h, R_E1 + h, sib)

        @pl.when(k > 0)
        def _():
            remain = state[0]
            tangents = []
            for i in range(2):
                high, low = split_high_low(remain[i * RANK : (i + 1) * RANK])
                stacked = jnp.concatenate([high, low, high], axis=0)
                tangents.append((ADAPTER_SCALE * dot(u3[i], stacked)).astype(BF16))
            dq, dv = tangents
            for h in range(HEADS):
                lanes = slice(h * HEAD_DIM, (h + 1) * HEAD_DIM)
                scores = dot_t(dq[:, lanes], k_ref[:, lanes]) * HEAD_DIM ** (-0.5)
                probs = pf[h]
                tilted = probs * scores
                dprobs = tilted - probs * jnp.sum(tilted, axis=-1, keepdims=True)
                left = jnp.concatenate([dprobs.astype(BF16), pb[h]], axis=1)
                right = jnp.concatenate([v_ref[:, lanes], dv[:, lanes]], axis=0)
                dmixed = dot(left, right).astype(BF16)
                dmcat[:, lanes] = dmixed
                e1s[h] = dmixed.astype(F32)
                e1(h).start()

        @pl.when(k == 0)
        def _():
            for h in range(HEADS):
                e1(h).start()

        sca[4] = jnp.broadcast_to(total(state[0] * state[0]), (8, 128))
        sca[5] = jnp.broadcast_to(total(state[0] * state[1]), (8, 128))
        s1 = remote(sca.at[pl.ds(4, 2)], s1r, S_S1, R_S1, sib)
        s1.start()
        for h in range(HEADS):
            e1(h).wait_recv()
            dmcat[:, pl.ds(COLS + h * HEAD_DIM, HEAD_DIM)] = e1r[h].astype(BF16)
        s1.wait_recv()
        sca[pl.ds(6, 2)] = sca[pl.ds(4, 2)] + s1r[...]
        s2 = remote(sca.at[pl.ds(6, 2)], s2r, S_S2, R_S2, xn)
        s2.start()

        def zi(off):
            return lax.rem(z + off, N_Z)

        def x1(s):
            return remote(part_x.at[s, 1 - x], rx1.at[s], S_X1 + s, R_X1 + s, xn)

        def z1(s, off):
            i = 3 * s + off - 1
            return remote(part_z.at[s, zi(off)], rz1.at[s, off - 1], S_Z1 + i, R_Z1 + i, zn(off))

        def x2(s, off):
            i = 3 * s + off - 1
            return remote(part_x.at[s, x, zi(off)], rx2.at[s, off - 1], S_X2 + i, R_X2 + i, zn(off))

        def z2(s):
            return remote(part_z.at[s, z], rz2.at[s], S_Z2 + s, R_Z2 + s, xn)

        for s in range(STAGES):
            for off in (2, 1, 3, 0):
                product = dot(dmcat[...], wb[s * N_Z + zi(off)])
                part_z[s, zi(off)] = product[:, LANES:]
                if off:
                    z1(s, off).start()
                part_x[s, 0, zi(off)] = product[:HALF, :LANES]
                part_x[s, 1, zi(off)] = product[HALF:, :LANES]
            x1(s).start()

        s2.wait_recv()
        s3b[z] = sca[pl.ds(6, 2)] + s2r[...]

        def s3(off, peer):
            return remote(s3b.at[peer], s3b.at[peer], S_S3 + off - 1, R_S3 + peer, zn(off))

        for off in (2, 1, 3):
            s3(off, z).start()

        for s in range(STAGES):
            x1(s).wait_recv()
            part_x[s, x] = part_x[s, x] + rx1[s]
            for off in (2, 1, 3):
                x2(s, off).start()
            for off in (1, 2, 3):
                z1(s, off).wait_recv()
            part_z[s, z] = part_z[s, z] + rz1[s, 0] + rz1[s, 1] + rz1[s, 2]
            z2(s).start()

        for off in (1, 2, 3):
            s3(off, zi(off)).wait_recv()
        sums = s3b[0] + s3b[1] + s3b[2] + s3b[3]
        sca[0] = sums[0]
        ratio = sums[0] / jnp.where(k > 1, sca[1], 1.0)
        beta = jnp.where(k == 0, 1.0, jnp.where(k == 1, 0.0, ratio))
        beta_row = beta[0:1, 0:1]
        sca[2] = sums[0] + 2.0 * beta * sums[1] + beta * beta * sca[2]

        def x3(s, off, peer):
            block = gx.at[s, x, peer]
            return remote(block, block, S_X3 + 3 * s + off - 1, R_X3 + N_Z * s + peer, zn(off))

        def x4(s, half):
            return remote(gx.at[s, half], gx.at[s, half], S_X4 + s, R_X4 + s, xn)

        def z4(s, off, peer):
            block = gz.at[s, peer]
            return remote(block, block, S_Z4 + 3 * s + off - 1, R_Z4 + N_Z * s + peer, zn(off))

        def own_x(s):
            for off in (1, 2, 3):
                x2(s, off).wait_recv()
            block = part_x[s, x, z] + rx2[s, 0] + rx2[s, 1] + rx2[s, 2]
            block = block * mask_x + beta_row * cprev_x[s]
            cprev_x[s] = block
            gx[s, x, z] = block
            for off in (2, 1, 3):
                x3(s, off, z).start()

        def own_z(s):
            z2(s).wait_recv()
            block = part_z[s, z] + rz2[s]
            block = block * mask_z + beta_row * cprev_z[s]
            cprev_z[s] = block
            gz[s, z] = block
            for off in (2, 1, 3):
                z4(s, off, z).start()

        own_x(0)
        own_x(1)
        own_z(0)
        own_x(2)
        own_z(1)
        own_z(2)
        state[1] = state[0] + beta_row * state[1]
        for s in range(STAGES):
            for off in (1, 3, 2):
                x3(s, off, zi(off)).wait_recv()
            x4(s, x).start()

        squares[...] = jnp.zeros_like(squares)
        for s in range(STAGES):
            x4(s, 1 - x).wait_recv()
            for off in (0, 1, 3, 2):
                if off:
                    z4(s, off, zi(off)).wait_recv()
                left = jnp.concatenate([gx[s, 0, zi(off)], gx[s, 1, zi(off)]], axis=0)
                both = jnp.concatenate([left, gz[s, zi(off)]], axis=1)
                product = dot_t(both.astype(BF16), wb[s * N_Z + zi(off)])
                if s == 0 and off == 0:
                    cot[...] = product
                else:
                    cot[...] = cot[...] + product
                squares[...] = squares[...] + both * both

        e2 = remote(cot.at[:, pl.ds(COLS, COLS)], e2r, S_E2, R_E2, sib)
        e2.start()
        sca[3] = jnp.broadcast_to(total(squares[...]), (8, 128))
        s6 = remote(sca.at[3], s6r, S_S6, R_S6, sib)
        s6.start()
        s6.wait_recv()

        parity = lax.rem(k, 2)

        def ar(i, peer):
            block = arb.at[parity, peer]
            r = R_AR + parity * N_DP + peer
            return remote(block, block, S_AR + i, r, (dpn(PEERS[i]), t))

        def sq(i, peer):
            block = sqb.at[parity, peer]
            r = R_SQ + parity * N_DP + peer
            return remote(block, block, S_SQ + i, r, (dpn(PEERS[i]), t))

        sqb[parity, d] = sca[3] + s6r[...]
        for i in range(N_DP - 1):
            sq(i, d).start()
        e2.wait_recv()
        for h in range(HEADS):
            lanes = slice(h * HEAD_DIM, (h + 1) * HEAD_DIM)
            cotan = (cot[:, lanes] + e2r[:, lanes]).astype(BF16)
            dprobs = dot_t(cotan, v_ref[:, lanes])
            probs = pf[h]
            tilted = probs * dprobs
            dscores = tilted - probs * jnp.sum(tilted, axis=-1, keepdims=True)
            dscores = (dscores * HEAD_DIM ** (-0.5)).astype(BF16)
            dq = dot(dscores, k_ref[:, lanes]).astype(BF16)
            dv = dot(pbt[h], cotan).astype(BF16)
            for i, cotangent in enumerate((dq, dv)):
                both = dot(ut[i], cotangent)
                arb[parity, d, i * RANK : (i + 1) * RANK, lanes] = ADAPTER_SCALE * (
                    both[:RANK] + both[RANK:]
                )
        for i in range(N_DP - 1):
            ar(i, d).start()

        for h in range(HEADS):
            e1(h).wait_send()
        s1.wait_send()
        s2.wait_send()
        for off in (1, 2, 3):
            s3(off, z).wait_send()
        for s in range(STAGES):
            x1(s).wait_send()
            z2(s).wait_send()
            x4(s, x).wait_send()
            for off in (1, 2, 3):
                z1(s, off).wait_send()
                x2(s, off).wait_send()
                x3(s, off, z).wait_send()
                z4(s, off, z).wait_send()
        e2.wait_send()
        s6.wait_send()

        for i in reversed(range(N_DP - 1)):
            ar(i, dpn(PEERS[i])).wait_recv()
            sq(i, dpn(PEERS[i])).wait_recv()
        for i in range(N_DP - 1):
            ar(i, d).wait_send()
            sq(i, d).wait_send()
        summed = arb[parity, 0]
        for peer in range(1, N_DP):
            summed = summed + arb[parity, peer]
        image = summed * (1.0 / (ROWS * N_DP)) + DAMP * state[1]
        squared = sqb[parity, 0]
        for peer in range(1, N_DP):
            squared = squared + sqb[parity, peer]
        squared = squared * (1.0 / (ROWS * N_DP))
        curvature = squared + DAMP * sca[2]
        alpha = jnp.where(k == 0, 1.0, sca[0] / jnp.where(k == 0, 1.0, curvature))[0:1, 0:1]
        state[2] = state[2] + jnp.where(k == 0, 0.0, alpha) * state[1]
        state[0] = state[0] - alpha * image
        sca[1] = sca[0]

    step_ref[...] = state[2]
    remain_ref[...] = state[0]


def solve(lengths, q, k, v, uq, uv, gap_x, gap_z, w_out):
    vmem = pl.BlockSpec(memory_space=pltpu.VMEM)
    square = (HEADS, HEAD_DIM, HEAD_DIM)
    half_block = (HALF, LANES)
    block = (ROWS, LANES)
    scratch = [
        pltpu.VMEM((CHUNKS, 2 * COLS, PAIR), BF16),
        pltpu.VMEM((CHUNKS, COLS, PAIR), BF16),
        pltpu.VMEM((CHUNKS, COLS, PAIR), F32),
        pltpu.VMEM((CHUNKS, COLS, PAIR), F32),
        pltpu.VMEM(square, F32),
        pltpu.VMEM(square, BF16),
        pltpu.VMEM(square, BF16),
        pltpu.VMEM((2, ROWS, 3 * RANK), BF16),
        pltpu.VMEM((2, 2 * RANK, ROWS), BF16),
        pltpu.VMEM((ROWS, 2 * COLS), BF16),
        pltpu.VMEM(square, F32),
        pltpu.VMEM(square, F32),
        pltpu.VMEM((STAGES, 2, N_Z) + half_block, F32),
        pltpu.VMEM((STAGES, N_Z) + block, F32),
        pltpu.VMEM((STAGES, N_Z) + half_block, F32),
        pltpu.VMEM((STAGES, N_Z - 1) + block, F32),
        pltpu.VMEM((STAGES, N_Z - 1) + half_block, F32),
        pltpu.VMEM((STAGES,) + block, F32),
        pltpu.VMEM((STAGES, 2, N_Z) + half_block, F32),
        pltpu.VMEM((STAGES, N_Z) + block, F32),
        pltpu.VMEM((STAGES,) + half_block, F32),
        pltpu.VMEM((STAGES,) + block, F32),
        pltpu.VMEM((ROWS, 2 * COLS), F32),
        pltpu.VMEM((ROWS, COLS), F32),
        pltpu.VMEM((2, N_DP, 2 * RANK, COLS), F32),
        pltpu.VMEM((2, N_DP, 8, 128), F32),
        pltpu.VMEM((ROWS, PAIR), F32),
        pltpu.VMEM((3, 2 * RANK, COLS), F32),
        pltpu.VMEM((8, 8, 128), F32),
        pltpu.VMEM((2, 8, 128), F32),
        pltpu.VMEM((2, 8, 128), F32),
        pltpu.VMEM((N_Z, 2, 8, 128), F32),
        pltpu.VMEM((8, 128), F32),
        pltpu.SemaphoreType.DMA((2 * CHUNKS,)),
        pltpu.SemaphoreType.DMA((N_SEND,)),
        pltpu.SemaphoreType.DMA((N_RECV,)),
    ]
    shape = jax.ShapeDtypeStruct((2 * RANK, COLS), F32)
    return pl.pallas_call(
        kernel,
        out_shape=(shape, shape),
        in_specs=[pl.BlockSpec(memory_space=pltpu.SMEM)]
        + [vmem] * 9
        + [pl.BlockSpec(memory_space=pl.ANY)],
        out_specs=(vmem, vmem),
        scratch_shapes=scratch,
        compiler_params=pltpu.CompilerParams(
            collective_id=0, has_side_effects=True, vmem_limit_bytes=48 * 2**20
        ),
        cost_estimate=pl.CostEstimate(
            flops=8 * 2 * ROWS * WIDTH * COLS, bytes_accessed=8 * 2**20, transcendentals=0
        ),
        name="newton",
    )(lengths, q, k, v, uq, uv, uq.T, uv.T, gap_x, gap_z, w_out)


def layer_norm(rows, gain, bias):
    rows = rows.astype(F32)
    centred = rows - jnp.mean(rows, axis=-1, keepdims=True)
    spread = jnp.mean(centred * centred, axis=-1, keepdims=True)
    return (centred * lax.rsqrt(spread + EPS) * gain + bias).astype(BF16)


def on_device(
    inputs,
    targets,
    lengths,
    ln_gain,
    ln_bias,
    query_weight,
    w_key,
    value_weight,
    w_out,
    down_query,
    down_value,
    query_up_factor,
    value_up_factor,
):
    normed = layer_norm(inputs, ln_gain, ln_bias)
    downs = jnp.concatenate([down_query, down_value], axis=1)
    both = jnp.dot(normed, downs, preferred_element_type=F32)
    uq, uv = both[:, :RANK], both[:, RANK:]

    def project(weight, low, up):
        rows = jnp.dot(normed, weight, preferred_element_type=F32)
        if up is not None:
            rows = rows + ADAPTER_SCALE * jnp.dot(low, up, precision=lax.Precision.HIGHEST)
        return rows.astype(BF16)

    q = project(query_weight, uq, query_up_factor)
    k = project(w_key, None, None)
    v = project(value_weight, uv, value_up_factor)

    t = lax.axis_index("tensor")
    gaps_x, gaps_z = [], []
    for s in range(STAGES):
        left = t % 2 * CORE_WIDTH + (s * N_Z + t // 4) * PAIR
        top = (t // 2) % 2 * HALF
        for gaps, size, at in (
            (gaps_x, (HALF, LANES), (top, left)),
            (gaps_z, (ROWS, LANES), (0, left + LANES)),
        ):
            parts = [lax.dynamic_slice(a, at, size) for a in (inputs, targets)]
            gaps.append(parts[0].astype(F32) - parts[1].astype(F32))
    step, remain = solve(lengths, q, k, v, uq, uv, jnp.stack(gaps_x), jnp.stack(gaps_z), w_out)
    return (step[:RANK], step[RANK:], remain[:RANK], remain[RANK:])


def solution(mesh):
    in_specs = (
        P("dp", None),
        P("dp", None),
        P("dp"),
        P(),
        P(),
        P(None, "tensor"),
        P(None, "tensor"),
        P(None, "tensor"),
        P("tensor", None),
        P(),
        P(),
        P(None, "tensor"),
        P(None, "tensor"),
    )
    out_specs = (P(None, "tensor"), P(None, "tensor"), P(None, "tensor"), P(None, "tensor"))
    return jax.shard_map(
        on_device, mesh=mesh, in_specs=in_specs, out_specs=out_specs, check_vma=False
    )
```

```python
import jax
import jax.numpy as jnp
from jax import lax
from jax.experimental import pallas as pl
from jax.experimental.pallas import tpu as pltpu
from jax.sharding import PartitionSpec as P

HEAD_DIM = 128
CG_STEPS = 3
HEADS = 3
COLS = HEADS * HEAD_DIM
ROWS = 128
HALF = ROWS // 2
RANK = 16
WIDTH = 6144
CORE_WIDTH = WIDTH // 2
STAGES = 3
LANES = 128
PAIR = 2 * LANES
CHUNKS = CORE_WIDTH // PAIR
N_DP = 8
N_Z = 4
DEPTH = 768

EPS = 1e-05
ADAPTER_SCALE = 2.0
DAMP = 0.05
NEG = -1e30

F32 = jnp.float32
BF16 = jnp.bfloat16
MESH = pl.DeviceIdType.MESH

S_W, S_E1, S_S1, S_S2, S_S3, S_S6, S_E2, S_X1, S_Z1, S_X2 = 0, 12, 15, 16, 17, 20, 21, 22, 25, 43
S_Z2, S_X3, S_X4, S_Z4, S_AR, S_SQ, N_SEND = 52, 55, 64, 76, 88, 95, 102
R_W, R_E1, R_S1, R_S2, R_S3, R_S6, R_E2, R_X1, R_Z1, R_X2 = 0, 12, 15, 16, 17, 21, 22, 23, 26, 44
R_Z2, R_X3, R_X4, R_Z4, R_AR, R_SQ, N_RECV = 53, 56, 68, 80, 92, 108, 124

PEERS = ((1, 2), (1, 1), (1, 3), (0, 2), (1, 0), (0, 1), (0, 3))


def dot(a, b):
    return lax.dot_general(a, b, (((1,), (0,)), ((), ())), preferred_element_type=F32)


def dot_t(a, b):
    return lax.dot_general(a, b, (((1,), (1,)), ((), ())), preferred_element_type=F32)


def split_high_low(x):
    high = x.astype(BF16)
    return high, (x - high.astype(F32)).astype(BF16)


def total(x):
    return jnp.sum(jnp.sum(x, axis=1, keepdims=True), axis=0, keepdims=True)


def kernel(
    len_ref,
    gain_ref,
    bias_ref,
    bq_ref,
    bv_ref,
    inputs_ref,
    targets_ref,
    wq_ref,
    wk_ref,
    wv_ref,
    dq_ref,
    dv_ref,
    w_ref,
    step_ref,
    remain_ref,
    inputs_v,
    targets_x,
    targets_z,
    normed,
    weights_v,
    rows_v,
    down_v,
    q_ref,
    k_ref,
    v_ref,
    wb,
    wtmp,
    wsend,
    wrecv,
    pf,
    pb,
    pbt,
    u3,
    ut,
    dmcat,
    e1s,
    e1r,
    part_x,
    part_z,
    rx1,
    rz0,
    rz1,
    rx2,
    rz2,
    gx,
    gz,
    cprev_x,
    cprev_z,
    cot,
    e2r,
    arb,
    sqb,
    squares,
    state,
    sca,
    s1r,
    s2r,
    s3b,
    s6r,
    lsem,
    psem,
    ssem,
    rsem,
):
    d = lax.axis_index("dp")
    t = lax.axis_index("tensor")
    c = lax.rem(t, 2)
    x = lax.rem(t // 2, 2)
    z = t // 4
    sib = (d, t + 1 - 2 * c)
    xn = (d, t + 2 - 4 * x)

    def zn(off):
        return (d, lax.rem(t + 4 * off, 16))

    def dpn(hop):
        return lax.rem(d // 4 + hop[0], 2) * 4 + lax.rem(d + hop[1], 4)

    def remote(src, dst, s, r, device):
        return pltpu.make_async_remote_copy(
            src_ref=src,
            dst_ref=dst,
            send_sem=ssem.at[s],
            recv_sem=rsem.at[r],
            device_id=device,
            device_id_type=MESH,
        )

    barrier = pltpu.get_barrier_semaphore()
    partners = [sib, xn] + [zn(o) for o in (1, 2, 3)] + [(dpn(hop), t) for hop in PEERS]
    for device in partners:
        pl.semaphore_signal(barrier, inc=1, device_id=device, device_id_type=MESH)

    def own_copy(j):
        columns = pl.ds(pl.multiple_of(c * CORE_WIDTH + j * PAIR, PAIR), PAIR)
        return pltpu.make_async_copy(
            w_ref.at[:, columns], wb.at[j, pl.ds(0, COLS)], lsem.at[j]
        )

    def other_copy(j):
        columns = pl.ds(pl.multiple_of((1 - c) * CORE_WIDTH + j * PAIR, PAIR), PAIR)
        return pltpu.make_async_copy(w_ref.at[:, columns], wtmp.at[j], lsem.at[CHUNKS + j])

    def w_copy(j):
        return remote(wsend.at[j], wrecv.at[j], S_W + j, R_W + j, sib)

    def order(i):
        return i // N_Z * N_Z + lax.rem(z + lax.rem(i + 2, N_Z), N_Z)

    def load(source, target, pieces, first):
        rows = source.shape[0] // pieces
        return [
            pltpu.make_async_copy(
                source.at[pl.ds(i * rows, rows)], target.at[pl.ds(i * rows, rows)], psem.at[first + i]
            )
            for i in range(pieces)
        ]

    load_inputs = load(inputs_ref, inputs_v, 4, 0)
    load_downs = [
        pltpu.make_async_copy(ref, down_v.at[pl.ds(i * RANK, RANK)], psem.at[4 + i])
        for i, ref in enumerate((dq_ref, dv_ref))
    ]
    half_rows = pl.ds(pl.multiple_of(x * HALF, HALF), HALF)

    def gap_lanes(s, region):
        left = c * CORE_WIDTH + (s * N_Z + z) * PAIR + region * LANES
        return pl.ds(pl.multiple_of(left, LANES), LANES)

    load_targets = []
    for s in range(STAGES):
        for i, (rows, target) in enumerate(((half_rows, targets_x), (pl.ds(0, ROWS), targets_z))):
            source = targets_ref.at[rows, gap_lanes(s, i)]
            load_targets.append(
                pltpu.make_async_copy(source, target.at[s], psem.at[6 + 2 * s + i])
            )

    def load_weights(i):
        rows = pl.ds(i * DEPTH, DEPTH)
        return [
            pltpu.make_async_copy(
                ref.at[rows],
                weights_v.at[rows, pl.ds(n * COLS, COLS)],
                psem.at[12 + 3 * i + n],
            )
            for n, ref in enumerate((wq_ref, wk_ref, wv_ref))
        ]

    pieces = [load_weights(i) for i in range(WIDTH // DEPTH)]
    for copy in load_inputs:
        copy.start()

    @pl.loop(0, CHUNKS)
    def _(i):
        other_copy(order(i)).start()

    for copy in load_downs + sum(pieces[:4], []):
        copy.start()

    for i, copy in enumerate(load_inputs):
        copy.wait()
        if i < 2:
            for late in pieces[4 + 2 * i] + pieces[5 + 2 * i]:
                late.start()
        if i == 2:

            @pl.loop(0, CHUNKS)
            def _(j):
                own_copy(order(j)).start()

            for late in load_targets:
                late.start()

        size = ROWS // len(load_inputs)

        @pl.loop(i * size // 16, (i + 1) * size // 16)
        def _(r):
            rows = pl.ds(pl.multiple_of(r * 16, 16), 16)
            wide = inputs_v[rows, :].astype(F32)
            centred = wide - jnp.sum(wide, axis=1, keepdims=True) * (1.0 / WIDTH)
            spread = jnp.sum(centred * centred, axis=1, keepdims=True) * (1.0 / WIDTH)
            scaled = centred * lax.rsqrt(spread + EPS)
            normed[rows, :] = (scaled * gain_ref[...] + bias_ref[...]).astype(BF16)

    pl.semaphore_wait(barrier, len(partners))

    @pl.loop(0, CHUNKS)
    def _(i):
        j = order(i)
        other_copy(j).wait()
        wsend[j] = wtmp[j].astype(F32)
        w_copy(j).start()

    for i, piece in enumerate(pieces):
        for copy in piece:
            copy.wait()
        depth = pl.ds(i * DEPTH, DEPTH)
        product = dot(normed[:, depth], weights_v[depth, :])
        rows_v[...] = product if i == 0 else rows_v[...] + product
    for copy in load_downs:
        copy.wait()
    lows = dot_t(normed[...], down_v[...])
    lows_t = lows.T
    k_ref[...] = rows_v[:, COLS : 2 * COLS].astype(BF16)
    for i, (target, up) in enumerate(((q_ref, bq_ref), (v_ref, bv_ref))):
        ranks = slice(i * RANK, (i + 1) * RANK)
        high, rest = split_high_low(lows[:, ranks])
        u3[i] = jnp.concatenate([high, high, rest], axis=1)
        high, rest = split_high_low(lows_t[ranks])
        ut[i] = jnp.concatenate([high, rest], axis=0)
        high, rest = split_high_low(up[...])
        stacked = jnp.concatenate([high, rest, high], axis=0)
        rows = rows_v[:, 2 * i * COLS : (2 * i + 1) * COLS]
        target[...] = (rows + ADAPTER_SCALE * dot(u3[i], stacked)).astype(BF16)

    limit = len_ref[0]
    row = lax.broadcasted_iota(jnp.int32, (ROWS, ROWS), 0)
    col = lax.broadcasted_iota(jnp.int32, (ROWS, ROWS), 1)
    live = (col <= row) & (col < limit)
    for h in range(HEADS):
        lanes = pl.ds(h * HEAD_DIM, HEAD_DIM)
        scores = dot_t(q_ref[:, lanes], k_ref[:, lanes]) * HEAD_DIM ** (-0.5)
        scores = jnp.where(live, scores, NEG)
        weights = jnp.exp(scores - jnp.max(scores, axis=-1, keepdims=True))
        probs = weights / jnp.sum(weights, axis=-1, keepdims=True)
        pf[h] = probs
        pb[h] = probs.astype(BF16)
        pbt[h] = probs.T.astype(BF16)
        mixed = dot(probs.astype(BF16), v_ref[:, lanes]).astype(BF16)
        dmcat[:, lanes] = mixed
        e1s[h] = mixed.astype(F32)
    place = lax.broadcasted_iota(jnp.int32, (ROWS, LANES), 0)
    mask_z = (place < limit).astype(F32)
    mask_x = (place[:HALF] + x * HALF < limit).astype(F32)
    for copy in load_targets:
        copy.wait()
    for s in range(STAGES):
        gap = inputs_v[half_rows, gap_lanes(s, 0)].astype(F32) - targets_x[s].astype(F32)
        cprev_x[s] = gap * mask_x
        gap = inputs_v[:, gap_lanes(s, 1)].astype(F32) - targets_z[s].astype(F32)
        cprev_z[s] = gap * mask_z
    state[...] = jnp.zeros_like(state)
    sca[...] = jnp.zeros_like(sca)

    @pl.loop(0, CG_STEPS + 1)
    def _(k):
        def e1(h):
            return remote(e1s.at[h], e1r.at[h], S_E1 + h, R_E1 + h, sib)

        @pl.when(k > 0)
        def _():
            remain = state[0]
            tangents = []
            for i in range(2):
                high, low = split_high_low(remain[i * RANK : (i + 1) * RANK])
                stacked = jnp.concatenate([high, low, high], axis=0)
                tangents.append((ADAPTER_SCALE * dot(u3[i], stacked)).astype(BF16))
            dq, dv = tangents
            for h in range(HEADS):
                lanes = slice(h * HEAD_DIM, (h + 1) * HEAD_DIM)
                scores = dot_t(dq[:, lanes], k_ref[:, lanes]) * HEAD_DIM ** (-0.5)
                probs = pf[h]
                tilted = probs * scores
                dprobs = tilted - probs * jnp.sum(tilted, axis=-1, keepdims=True)
                left = jnp.concatenate([dprobs.astype(BF16), pb[h]], axis=1)
                right = jnp.concatenate([v_ref[:, lanes], dv[:, lanes]], axis=0)
                dmixed = dot(left, right).astype(BF16)
                dmcat[:, lanes] = dmixed
                e1s[h] = dmixed.astype(F32)
                e1(h).start()

        @pl.when(k == 0)
        def _():
            for h in range(HEADS):
                e1(h).start()

        sca[4] = jnp.broadcast_to(total(state[0] * state[0]), (8, 128))
        sca[5] = jnp.broadcast_to(total(state[0] * state[1]), (8, 128))
        s1 = remote(sca.at[pl.ds(4, 2)], s1r, S_S1, R_S1, sib)
        s1.start()
        for h in range(HEADS):
            e1(h).wait_recv()
            dmcat[:, pl.ds(COLS + h * HEAD_DIM, HEAD_DIM)] = e1r[h].astype(BF16)
        s1.wait_recv()
        sca[pl.ds(6, 2)] = sca[pl.ds(4, 2)] + s1r[...]
        s2 = remote(sca.at[pl.ds(6, 2)], s2r, S_S2, R_S2, xn)
        s2.start()

        def zi(off):
            return lax.rem(z + off, N_Z)

        def x1(s):
            return remote(part_x.at[s, 1 - x], rx1.at[s], S_X1 + s, R_X1 + s, xn)

        upper, lower = pl.ds(0, HALF), pl.ds(HALF, HALF)

        def z1(s, role):
            to, row, target = (
                (2, upper, rz0.at[s, 0]),
                (2, lower, rz0.at[s, 1]),
                (1, lower, rz1.at[s, 0, lower]),
                (3, upper, rz1.at[s, 1, upper]),
                (1, upper, rz1.at[s, 0, upper]),
                (3, lower, rz1.at[s, 1, lower]),
            )[role]
            i = 6 * s + role
            source = part_z.at[s, zi(to), row]
            return remote(source, target, S_Z1 + i, R_Z1 + i, zn(1 if role % 2 == 0 else 3))

        def x2(s, off):
            i = 3 * s + off - 1
            return remote(part_x.at[s, x, zi(off)], rx2.at[s, off - 1], S_X2 + i, R_X2 + i, zn(off))

        def z2(s):
            return remote(part_z.at[s, z], rz2.at[s], S_Z2 + s, R_Z2 + s, xn)

        for s in range(STAGES):

            @pl.when(k == 0)
            def _():
                for off in (2, 3, 0, 1):
                    j = s * N_Z + zi(off)
                    own_copy(j).wait()
                    w_copy(j).wait_recv()
                    wb[j, pl.ds(COLS, COLS)] = wrecv[j].astype(BF16)

            for off in (2, 1, 3, 0):
                product = dot(dmcat[...], wb[s * N_Z + zi(off)])
                part_z[s, zi(off)] = product[:, LANES:]
                for role in ((), (2,), (0, 1), (3,))[off]:
                    z1(s, role).start()
                part_x[s, 0, zi(off)] = product[:HALF, :LANES]
                part_x[s, 1, zi(off)] = product[HALF:, :LANES]
            x1(s).start()

        s2.wait_recv()
        s3b[z] = sca[pl.ds(6, 2)] + s2r[...]

        def s3(off, peer):
            return remote(s3b.at[peer], s3b.at[peer], S_S3 + off - 1, R_S3 + peer, zn(off))

        for off in (2, 1, 3):
            s3(off, z).start()

        for s in range(STAGES):
            z1(s, 0).wait_recv()
            part_z[s, zi(1), :HALF] = part_z[s, zi(1), :HALF] + rz0[s, 0]
            z1(s, 4).start()
            z1(s, 1).wait_recv()
            part_z[s, zi(3), HALF:] = part_z[s, zi(3), HALF:] + rz0[s, 1]
            z1(s, 5).start()

        def second_x(s):
            x1(s).wait_recv()
            part_x[s, x] = part_x[s, x] + rx1[s]
            for off in (2, 1, 3):
                x2(s, off).start()

        def second_z(s):
            for role in (2, 3, 4, 5):
                z1(s, role).wait_recv()
            part_z[s, z] = part_z[s, z] + rz1[s, 0] + rz1[s, 1]
            z2(s).start()

        second_x(0)
        second_z(0)
        second_x(1)
        second_z(1)
        second_z(2)
        second_x(2)

        for off in (1, 2, 3):
            s3(off, zi(off)).wait_recv()
        sums = s3b[0] + s3b[1] + s3b[2] + s3b[3]
        sca[0] = sums[0]
        ratio = sums[0] / jnp.where(k > 1, sca[1], 1.0)
        beta = jnp.where(k == 0, 1.0, jnp.where(k == 1, 0.0, ratio))
        beta_row = beta[0:1, 0:1]
        sca[2] = sums[0] + 2.0 * beta * sums[1] + beta * beta * sca[2]

        def x3(s, off, peer):
            block = gx.at[s, x, peer]
            return remote(block, block, S_X3 + 3 * s + off - 1, R_X3 + N_Z * s + peer, zn(off))

        def x4(s, half, peer):
            block = gx.at[s, half, peer]
            i = N_Z * s + peer
            return remote(block, block, S_X4 + i, R_X4 + i, xn)

        def z4(s, role, incoming=False):
            if incoming:
                block = (
                    gz.at[s, zi(3)],
                    gz.at[s, zi(1)],
                    gz.at[s, zi(2), upper],
                    gz.at[s, zi(2), lower],
                )[role]
            else:
                block = (
                    gz.at[s, z],
                    gz.at[s, z],
                    gz.at[s, zi(3), upper],
                    gz.at[s, zi(1), lower],
                )[role]
            i = 4 * s + role
            return remote(block, block, S_Z4 + i, R_Z4 + i, zn(1 if role % 2 == 0 else 3))

        def own_x(s):
            for off in (1, 2, 3):
                x2(s, off).wait_recv()
            block = part_x[s, x, z] + rx2[s, 0] + rx2[s, 1] + rx2[s, 2]
            block = block * mask_x + beta_row * cprev_x[s]
            cprev_x[s] = block
            gx[s, x, z] = block
            for off in (2, 1, 3):
                x3(s, off, z).start()
            x4(s, x, z).start()

        def own_z(s):
            z2(s).wait_recv()
            block = part_z[s, z] + rz2[s]
            block = block * mask_z + beta_row * cprev_z[s]
            cprev_z[s] = block
            gz[s, z] = block
            z4(s, 0).start()
            z4(s, 1).start()

        def pass_x(s):
            for off in (1, 3, 2):
                x3(s, off, zi(off)).wait_recv()
                x4(s, x, zi(off)).start()

        def pass_z(s):
            for role in range(2):
                z4(s, role, True).wait_recv()
                z4(s, role + 2).start()

        own_x(0)
        own_z(0)
        own_x(1)
        own_z(1)
        own_z(2)
        pass_x(0)
        own_x(2)
        state[1] = state[0] + beta_row * state[1]
        pass_z(0)
        pass_x(1)
        pass_z(1)
        pass_z(2)
        pass_x(2)

        squares[...] = jnp.zeros_like(squares)
        for s in range(STAGES):
            for off in (0, 1, 3, 2):
                x4(s, 1 - x, zi(off)).wait_recv()
                if off == 2:
                    z4(s, 2, True).wait_recv()
                    z4(s, 3, True).wait_recv()
                left = jnp.concatenate([gx[s, 0, zi(off)], gx[s, 1, zi(off)]], axis=0)
                both = jnp.concatenate([left, gz[s, zi(off)]], axis=1)
                product = dot_t(both.astype(BF16), wb[s * N_Z + zi(off)])
                if s == 0 and off == 0:
                    cot[...] = product
                else:
                    cot[...] = cot[...] + product
                squares[...] = squares[...] + both * both

        e2 = remote(cot.at[:, pl.ds(COLS, COLS)], e2r, S_E2, R_E2, sib)
        e2.start()
        sca[3] = jnp.broadcast_to(total(squares[...]), (8, 128))
        s6 = remote(sca.at[3], s6r, S_S6, R_S6, sib)
        s6.start()
        s6.wait_recv()

        parity = lax.rem(k, 2)

        def ar(i, peer):
            block = arb.at[parity, peer]
            r = R_AR + parity * N_DP + peer
            return remote(block, block, S_AR + i, r, (dpn(PEERS[i]), t))

        def sq(i, peer):
            block = sqb.at[parity, peer]
            r = R_SQ + parity * N_DP + peer
            return remote(block, block, S_SQ + i, r, (dpn(PEERS[i]), t))

        sqb[parity, d] = sca[3] + s6r[...]
        for i in range(N_DP - 1):
            sq(i, d).start()
        e2.wait_recv()
        for h in range(HEADS):
            lanes = slice(h * HEAD_DIM, (h + 1) * HEAD_DIM)
            cotan = (cot[:, lanes] + e2r[:, lanes]).astype(BF16)
            dprobs = dot_t(cotan, v_ref[:, lanes])
            probs = pf[h]
            tilted = probs * dprobs
            dscores = tilted - probs * jnp.sum(tilted, axis=-1, keepdims=True)
            dscores = (dscores * HEAD_DIM ** (-0.5)).astype(BF16)
            dq = dot(dscores, k_ref[:, lanes]).astype(BF16)
            dv = dot(pbt[h], cotan).astype(BF16)
            for i, cotangent in enumerate((dq, dv)):
                both = dot(ut[i], cotangent)
                arb[parity, d, i * RANK : (i + 1) * RANK, lanes] = ADAPTER_SCALE * (
                    both[:RANK] + both[RANK:]
                )
        for i in range(N_DP - 1):
            ar(i, d).start()

        for h in range(HEADS):
            e1(h).wait_send()
        s1.wait_send()
        s2.wait_send()
        for off in (1, 2, 3):
            s3(off, z).wait_send()
        for s in range(STAGES):
            x1(s).wait_send()
            z2(s).wait_send()
            for off in (1, 2, 3):
                x2(s, off).wait_send()
                x3(s, off, z).wait_send()
            for peer in range(N_Z):
                x4(s, x, peer).wait_send()
                z4(s, peer).wait_send()
            for role in range(6):
                z1(s, role).wait_send()
        e2.wait_send()
        s6.wait_send()

        for i in reversed(range(N_DP - 1)):
            ar(i, dpn(PEERS[i])).wait_recv()
            sq(i, dpn(PEERS[i])).wait_recv()
        for i in range(N_DP - 1):
            ar(i, d).wait_send()
            sq(i, d).wait_send()
        summed = arb[parity, 0]
        for peer in range(1, N_DP):
            summed = summed + arb[parity, peer]
        image = summed * (1.0 / (ROWS * N_DP)) + DAMP * state[1]
        squared = sqb[parity, 0]
        for peer in range(1, N_DP):
            squared = squared + sqb[parity, peer]
        squared = squared * (1.0 / (ROWS * N_DP))
        curvature = squared + DAMP * sca[2]
        alpha = jnp.where(k == 0, 1.0, sca[0] / jnp.where(k == 0, 1.0, curvature))[0:1, 0:1]
        state[2] = state[2] + jnp.where(k == 0, 0.0, alpha) * state[1]
        state[0] = state[0] - alpha * image
        sca[1] = sca[0]

    for j in range(CHUNKS):
        w_copy(j).wait_send()
    step_ref[...] = state[2]
    remain_ref[...] = state[0]


def solve(lengths, gain, bias, bq, bv, inputs, targets, wq, wk, wv, dq, dv, w_out):
    vmem = pl.BlockSpec(memory_space=pltpu.VMEM)
    square = (HEADS, HEAD_DIM, HEAD_DIM)
    half_block = (HALF, LANES)
    block = (ROWS, LANES)
    scratch = [
        pltpu.VMEM((ROWS, WIDTH), BF16),
        pltpu.VMEM((STAGES,) + half_block, BF16),
        pltpu.VMEM((STAGES,) + block, BF16),
        pltpu.VMEM((ROWS, WIDTH), BF16),
        pltpu.VMEM((WIDTH, 3 * COLS), BF16),
        pltpu.VMEM((ROWS, 3 * COLS), F32),
        pltpu.VMEM((2 * RANK, WIDTH), BF16),
        pltpu.VMEM((ROWS, COLS), BF16),
        pltpu.VMEM((ROWS, COLS), BF16),
        pltpu.VMEM((ROWS, COLS), BF16),
        pltpu.VMEM((CHUNKS, 2 * COLS, PAIR), BF16),
        pltpu.VMEM((CHUNKS, COLS, PAIR), BF16),
        pltpu.VMEM((CHUNKS, COLS, PAIR), F32),
        pltpu.VMEM((CHUNKS, COLS, PAIR), F32),
        pltpu.VMEM(square, F32),
        pltpu.VMEM(square, BF16),
        pltpu.VMEM(square, BF16),
        pltpu.VMEM((2, ROWS, 3 * RANK), BF16),
        pltpu.VMEM((2, 2 * RANK, ROWS), BF16),
        pltpu.VMEM((ROWS, 2 * COLS), BF16),
        pltpu.VMEM(square, F32),
        pltpu.VMEM(square, F32),
        pltpu.VMEM((STAGES, 2, N_Z) + half_block, F32),
        pltpu.VMEM((STAGES, N_Z) + block, F32),
        pltpu.VMEM((STAGES, N_Z) + half_block, F32),
        pltpu.VMEM((STAGES, 2) + half_block, F32),
        pltpu.VMEM((STAGES, 2) + block, F32),
        pltpu.VMEM((STAGES, N_Z - 1) + half_block, F32),
        pltpu.VMEM((STAGES,) + block, F32),
        pltpu.VMEM((STAGES, 2, N_Z) + half_block, F32),
        pltpu.VMEM((STAGES, N_Z) + block, F32),
        pltpu.VMEM((STAGES,) + half_block, F32),
        pltpu.VMEM((STAGES,) + block, F32),
        pltpu.VMEM((ROWS, 2 * COLS), F32),
        pltpu.VMEM((ROWS, COLS), F32),
        pltpu.VMEM((2, N_DP, 2 * RANK, COLS), F32),
        pltpu.VMEM((2, N_DP, 8, 128), F32),
        pltpu.VMEM((ROWS, PAIR), F32),
        pltpu.VMEM((3, 2 * RANK, COLS), F32),
        pltpu.VMEM((8, 8, 128), F32),
        pltpu.VMEM((2, 8, 128), F32),
        pltpu.VMEM((2, 8, 128), F32),
        pltpu.VMEM((N_Z, 2, 8, 128), F32),
        pltpu.VMEM((8, 128), F32),
        pltpu.SemaphoreType.DMA((2 * CHUNKS,)),
        pltpu.SemaphoreType.DMA((36,)),
        pltpu.SemaphoreType.DMA((N_SEND,)),
        pltpu.SemaphoreType.DMA((N_RECV,)),
    ]
    shape = jax.ShapeDtypeStruct((2 * RANK, COLS), F32)
    return pl.pallas_call(
        kernel,
        out_shape=(shape, shape),
        in_specs=[pl.BlockSpec(memory_space=pltpu.SMEM)]
        + [vmem] * 4
        + [pl.BlockSpec(memory_space=pl.ANY)] * 8,
        out_specs=(vmem, vmem),
        scratch_shapes=scratch,
        compiler_params=pltpu.CompilerParams(
            collective_id=0, has_side_effects=True, vmem_limit_bytes=58 * 2**20
        ),
        cost_estimate=pl.CostEstimate(
            flops=8 * 2 * ROWS * WIDTH * COLS, bytes_accessed=8 * 2**20, transcendentals=0
        ),
        name="newton",
    )(lengths, gain, bias, bq, bv, inputs, targets, wq, wk, wv, dq, dv, w_out)


def on_device(
    inputs,
    targets,
    lengths,
    ln_gain,
    ln_bias,
    query_weight,
    w_key,
    value_weight,
    w_out,
    down_query,
    down_value,
    query_up_factor,
    value_up_factor,
):
    step, remain = solve(
        lengths,
        ln_gain.reshape(1, WIDTH),
        ln_bias.reshape(1, WIDTH),
        query_up_factor,
        value_up_factor,
        inputs,
        targets,
        query_weight,
        w_key,
        value_weight,
        down_query.T,
        down_value.T,
        w_out,
    )
    return (step[:RANK], step[RANK:], remain[:RANK], remain[RANK:])


def solution(mesh):
    in_specs = (
        P("dp", None),
        P("dp", None),
        P("dp"),
        P(),
        P(),
        P(None, "tensor"),
        P(None, "tensor"),
        P(None, "tensor"),
        P("tensor", None),
        P(),
        P(),
        P(None, "tensor"),
        P(None, "tensor"),
    )
    out_specs = (P(None, "tensor"), P(None, "tensor"), P(None, "tensor"), P(None, "tensor"))
    return jax.shard_map(
        on_device, mesh=mesh, in_specs=in_specs, out_specs=out_specs, check_vma=False
    )
```

```python
import jax
import jax.numpy as jnp
from jax import lax
from jax.experimental import pallas as pl
from jax.experimental.pallas import tpu as pltpu
from jax.sharding import PartitionSpec as P

HEAD_DIM = 128
CG_STEPS = 3
HEADS = 3
COLS = HEADS * HEAD_DIM
ROWS = 128
HALF = ROWS // 2
RANK = 16
WIDTH = 6144
CORE_WIDTH = WIDTH // 2
STAGES = 3
LANES = 128
PAIR = 2 * LANES
CHUNKS = CORE_WIDTH // PAIR
N_DP = 8
N_Z = 4
DEPTH = 768

EPS = 1e-05
ADAPTER_SCALE = 2.0
DAMP = 0.05
NEG = -1e30

F32 = jnp.float32
BF16 = jnp.bfloat16
MESH = pl.DeviceIdType.MESH

S_W, S_E1, S_S1, S_S2, S_S3, S_S6, S_E2, S_X1, S_Z1, S_X2 = 0, 12, 15, 16, 17, 20, 21, 22, 25, 43
S_Z2, S_X3, S_X4, S_Z4, S_AR, S_SQ, N_SEND = 52, 55, 64, 76, 88, 102, 109
R_W, R_E1, R_S1, R_S2, R_S3, R_S6, R_E2, R_X1, R_Z1, R_X2 = 0, 12, 15, 16, 17, 21, 22, 23, 26, 44
R_Z2, R_X3, R_X4, R_Z4, R_AR, R_SQ, N_RECV = 53, 56, 68, 80, 92, 124, 140

PEERS = ((1, 2), (1, 1), (1, 3), (0, 2), (1, 0), (0, 1), (0, 3))


def dot(a, b):
    return lax.dot_general(a, b, (((1,), (0,)), ((), ())), preferred_element_type=F32)


def dot_t(a, b):
    return lax.dot_general(a, b, (((1,), (1,)), ((), ())), preferred_element_type=F32)


def split_high_low(x):
    high = x.astype(BF16)
    return high, (x - high.astype(F32)).astype(BF16)


def total(x):
    return jnp.sum(jnp.sum(x, axis=1, keepdims=True), axis=0, keepdims=True)


def kernel(
    len_ref,
    gain_ref,
    bias_ref,
    bq_ref,
    bv_ref,
    inputs_ref,
    targets_ref,
    wq_ref,
    wk_ref,
    wv_ref,
    dq_ref,
    dv_ref,
    w_ref,
    step_ref,
    remain_ref,
    inputs_v,
    targets_x,
    targets_z,
    normed,
    weights_v,
    rows_v,
    down_v,
    q_ref,
    k_ref,
    v_ref,
    wb,
    wtmp,
    wsend,
    wrecv,
    pf,
    pb,
    pbt,
    u3,
    ut,
    dmcat,
    begun,
    e1s,
    e1r,
    part_x,
    part_z,
    rx1,
    rz0,
    rz1,
    rx2,
    rz2,
    gx,
    gz,
    cprev_x,
    cprev_z,
    cot,
    e2r,
    arb,
    sqb,
    squares,
    state,
    sca,
    s1r,
    s2r,
    s3b,
    s6r,
    lsem,
    psem,
    ssem,
    rsem,
):
    d = lax.axis_index("dp")
    t = lax.axis_index("tensor")
    c = lax.rem(t, 2)
    x = lax.rem(t // 2, 2)
    z = t // 4
    sib = (d, t + 1 - 2 * c)
    xn = (d, t + 2 - 4 * x)

    def zn(off):
        return (d, lax.rem(t + 4 * off, 16))

    def dpn(hop):
        return lax.rem(d // 4 + hop[0], 2) * 4 + lax.rem(d + hop[1], 4)

    def remote(src, dst, s, r, device):
        return pltpu.make_async_remote_copy(
            src_ref=src,
            dst_ref=dst,
            send_sem=ssem.at[s],
            recv_sem=rsem.at[r],
            device_id=device,
            device_id_type=MESH,
        )

    barrier = pltpu.get_barrier_semaphore()
    partners = [sib, xn] + [zn(o) for o in (1, 2, 3)] + [(dpn(hop), t) for hop in PEERS]
    for device in partners:
        pl.semaphore_signal(barrier, inc=1, device_id=device, device_id_type=MESH)

    def own_copy(j):
        columns = pl.ds(pl.multiple_of(c * CORE_WIDTH + j * PAIR, PAIR), PAIR)
        return pltpu.make_async_copy(
            w_ref.at[:, columns], wb.at[j, pl.ds(0, COLS)], lsem.at[j]
        )

    def other_copy(j):
        columns = pl.ds(pl.multiple_of((1 - c) * CORE_WIDTH + j * PAIR, PAIR), PAIR)
        return pltpu.make_async_copy(w_ref.at[:, columns], wtmp.at[j], lsem.at[CHUNKS + j])

    def w_copy(j):
        return remote(wsend.at[j], wrecv.at[j], S_W + j, R_W + j, sib)

    def order(i):
        return i // N_Z * N_Z + lax.rem(z + lax.rem(i + 2, N_Z), N_Z)

    def load(source, target, pieces, first):
        rows = source.shape[0] // pieces
        return [
            pltpu.make_async_copy(
                source.at[pl.ds(i * rows, rows)], target.at[pl.ds(i * rows, rows)], psem.at[first + i]
            )
            for i in range(pieces)
        ]

    load_inputs = load(inputs_ref, inputs_v, 4, 0)
    load_downs = [
        pltpu.make_async_copy(ref, down_v.at[pl.ds(i * RANK, RANK)], psem.at[4 + i])
        for i, ref in enumerate((dq_ref, dv_ref))
    ]
    half_rows = pl.ds(pl.multiple_of(x * HALF, HALF), HALF)

    def gap_lanes(s, region):
        left = c * CORE_WIDTH + (s * N_Z + z) * PAIR + region * LANES
        return pl.ds(pl.multiple_of(left, LANES), LANES)

    load_targets = []
    for s in range(STAGES):
        for i, (rows, target) in enumerate(((half_rows, targets_x), (pl.ds(0, ROWS), targets_z))):
            source = targets_ref.at[rows, gap_lanes(s, i)]
            load_targets.append(
                pltpu.make_async_copy(source, target.at[s], psem.at[6 + 2 * s + i])
            )

    def load_weights(i):
        rows = pl.ds(i * DEPTH, DEPTH)
        return [
            pltpu.make_async_copy(
                ref.at[rows],
                weights_v.at[rows, pl.ds(n * COLS, COLS)],
                psem.at[12 + 3 * i + n],
            )
            for n, ref in enumerate((wq_ref, wk_ref, wv_ref))
        ]

    pieces = [load_weights(i) for i in range(WIDTH // DEPTH)]
    for copy in load_inputs:
        copy.start()

    @pl.loop(0, CHUNKS)
    def _(i):
        other_copy(order(i)).start()

    for copy in load_downs + sum(pieces[:4], []):
        copy.start()

    for i, copy in enumerate(load_inputs):
        copy.wait()
        if i < 2:
            for late in pieces[4 + 2 * i] + pieces[5 + 2 * i]:
                late.start()
        if i == 2:

            @pl.loop(0, CHUNKS)
            def _(j):
                own_copy(order(j)).start()

            for late in load_targets:
                late.start()

        size = ROWS // len(load_inputs)

        @pl.loop(i * size // 16, (i + 1) * size // 16)
        def _(r):
            rows = pl.ds(pl.multiple_of(r * 16, 16), 16)
            wide = inputs_v[rows, :].astype(F32)
            centred = wide - jnp.sum(wide, axis=1, keepdims=True) * (1.0 / WIDTH)
            spread = jnp.sum(centred * centred, axis=1, keepdims=True) * (1.0 / WIDTH)
            scaled = centred * lax.rsqrt(spread + EPS)
            normed[rows, :] = (scaled * gain_ref[...] + bias_ref[...]).astype(BF16)

    pl.semaphore_wait(barrier, len(partners))

    for i, piece in enumerate(pieces):
        given = [order(j) for j in range(3 * i // 2, 3 * (i + 1) // 2)]
        for copy in piece + [other_copy(j) for j in given]:
            copy.wait()
        depth = pl.ds(i * DEPTH, DEPTH)
        product = dot(normed[:, depth], weights_v[depth, :])
        for j in given:
            wsend[j] = wtmp[j].astype(F32)
        rows_v[...] = product if i == 0 else rows_v[...] + product
        for j in given:
            w_copy(j).start()
    for copy in load_downs:
        copy.wait()
    lows = dot_t(normed[...], down_v[...])
    lows_t = lows.T
    k_ref[...] = rows_v[:, COLS : 2 * COLS].astype(BF16)
    for i, (target, up) in enumerate(((q_ref, bq_ref), (v_ref, bv_ref))):
        ranks = slice(i * RANK, (i + 1) * RANK)
        high, rest = split_high_low(lows[:, ranks])
        u3[i] = jnp.concatenate([high, high, rest], axis=1)
        high, rest = split_high_low(lows_t[ranks])
        ut[i] = jnp.concatenate([high, rest], axis=0)
        high, rest = split_high_low(up[...])
        stacked = jnp.concatenate([high, rest, high], axis=0)
        rows = rows_v[:, 2 * i * COLS : (2 * i + 1) * COLS]
        target[...] = (rows + ADAPTER_SCALE * dot(u3[i], stacked)).astype(BF16)

    limit = len_ref[0]
    row = lax.broadcasted_iota(jnp.int32, (ROWS, ROWS), 0)
    col = lax.broadcasted_iota(jnp.int32, (ROWS, ROWS), 1)
    live = (col <= row) & (col < limit)
    lanes = [pl.ds(h * HEAD_DIM, HEAD_DIM) for h in range(HEADS)]
    scores = [dot_t(q_ref[:, n], k_ref[:, n]) * HEAD_DIM ** (-0.5) for n in lanes]
    scores = [jnp.where(live, a, NEG) for a in scores]
    weights = [jnp.exp(a - jnp.max(a, axis=-1, keepdims=True)) for a in scores]
    probs = [a / jnp.sum(a, axis=-1, keepdims=True) for a in weights]
    mixed = [dot(a.astype(BF16), v_ref[:, n]).astype(BF16) for a, n in zip(probs, lanes)]
    for h, n in enumerate(lanes):
        pf[h] = probs[h]
        pb[h] = probs[h].astype(BF16)
        pbt[h] = probs[h].T.astype(BF16)
        dmcat[:, n] = mixed[h]
        e1s[:, n] = mixed[h].astype(F32)
    place = lax.broadcasted_iota(jnp.int32, (ROWS, LANES), 0)
    mask_z = (place < limit).astype(F32)
    mask_x = (place[:HALF] + x * HALF < limit).astype(F32)
    for copy in load_targets:
        copy.wait()
    for s in range(STAGES):
        gap = inputs_v[half_rows, gap_lanes(s, 0)].astype(F32) - targets_x[s].astype(F32)
        cprev_x[s] = gap * mask_x
        gap = inputs_v[:, gap_lanes(s, 1)].astype(F32) - targets_z[s].astype(F32)
        cprev_z[s] = gap * mask_z
    state[...] = jnp.zeros_like(state)
    sca[...] = jnp.zeros_like(sca)

    @pl.loop(0, CG_STEPS + 1)
    def _(k):
        @pl.when(k > 0)
        def _():
            tangents = []
            for i in range(2):
                high, low = split_high_low(state[0, i * RANK : (i + 1) * RANK])
                stacked = jnp.concatenate([high, low, high], axis=0)
                tangents.append((ADAPTER_SCALE * dot(u3[i], stacked)).astype(BF16))
            dq, dv = [[a[:, h * HEAD_DIM : (h + 1) * HEAD_DIM] for h in range(HEADS)] for a in tangents]
            scores = [dot_t(a, k_ref[:, n]) * HEAD_DIM ** (-0.5) for a, n in zip(dq, lanes)]
            tilted = [pf[h] * a for h, a in enumerate(scores)]
            dprobs = [
                (a - pf[h] * jnp.sum(a, axis=-1, keepdims=True)).astype(BF16)
                for h, a in enumerate(tilted)
            ]
            left = [jnp.concatenate([a, pb[h]], axis=1) for h, a in enumerate(dprobs)]
            right = [jnp.concatenate([v_ref[:, n], a], axis=0) for a, n in zip(dv, lanes)]
            dmixed = [dot(a, b).astype(BF16) for a, b in zip(left, right)]
            for a, n in zip(dmixed, lanes):
                e1s[:, n] = a.astype(F32)
                dmcat[:, n] = a

        e1 = remote(e1s, e1r, S_E1, R_E1, sib)
        e1.start()
        sca[4] = jnp.broadcast_to(total(state[0] * state[0]), (8, 128))
        sca[5] = jnp.broadcast_to(total(state[0] * state[1]), (8, 128))
        s1 = remote(sca.at[pl.ds(4, 2)], s1r, S_S1, R_S1, sib)
        s1.start()
        @pl.when(k == 0)
        def _():
            for j in range(CHUNKS):
                own_copy(j).wait()

        for s in range(STAGES):
            for off in (2, 1, 3, 0):
                begun[s, off] = dot(dmcat[:, :PAIR], wb[s * N_Z + lax.rem(z + off, N_Z), :PAIR])
        e1.wait_recv()
        dmcat[:, pl.ds(COLS, COLS)] = e1r[...].astype(BF16)
        s1.wait_recv()
        sca[pl.ds(6, 2)] = sca[pl.ds(4, 2)] + s1r[...]
        s2 = remote(sca.at[pl.ds(6, 2)], s2r, S_S2, R_S2, xn)
        s2.start()

        def zi(off):
            return lax.rem(z + off, N_Z)

        def x1(s):
            return remote(part_x.at[s, 1 - x], rx1.at[s], S_X1 + s, R_X1 + s, xn)

        upper, lower = pl.ds(0, HALF), pl.ds(HALF, HALF)

        def z1(s, role):
            to, row, target = (
                (2, upper, rz0.at[s, 0]),
                (2, lower, rz0.at[s, 1]),
                (1, pl.ds(0, ROWS), rz1.at[s, 0]),
                (3, pl.ds(0, ROWS), rz1.at[s, 1]),
            )[role]
            i = 4 * s + role
            source = part_z.at[s, zi(to), row]
            return remote(source, target, S_Z1 + i, R_Z1 + i, zn(1 if role % 2 == 0 else 3))

        def x2(s, off):
            i = 3 * s + off - 1
            return remote(part_x.at[s, x, zi(off)], rx2.at[s, off - 1], S_X2 + i, R_X2 + i, zn(off))

        def z2(s):
            return remote(part_z.at[s, z], rz2.at[s], S_Z2 + s, R_Z2 + s, xn)

        for s in range(STAGES):

            @pl.when(k == 0)
            def _():
                for off in (2, 3, 0, 1):
                    j = s * N_Z + zi(off)
                    w_copy(j).wait_recv()
                    wb[j, pl.ds(COLS, COLS)] = wrecv[j].astype(BF16)

            for off in (2, 1, 3, 0):
                product = begun[s, off] + dot(dmcat[:, PAIR:], wb[s * N_Z + zi(off), PAIR:])
                part_z[s, zi(off)] = product[:, LANES:]
                for role in (0, 1) if off == 2 else ():
                    z1(s, role).start()
                part_x[s, 0, zi(off)] = product[:HALF, :LANES]
                part_x[s, 1, zi(off)] = product[HALF:, :LANES]
            x1(s).start()

        s2.wait_recv()
        s3b[z] = sca[pl.ds(6, 2)] + s2r[...]

        def s3(off, peer):
            return remote(s3b.at[peer], s3b.at[peer], S_S3 + off - 1, R_S3 + peer, zn(off))

        for off in (2, 1, 3):
            s3(off, z).start()

        for s in range(STAGES):
            z1(s, 0).wait_recv()
            part_z[s, zi(1), :HALF] = part_z[s, zi(1), :HALF] + rz0[s, 0]
            z1(s, 2).start()
            z1(s, 1).wait_recv()
            part_z[s, zi(3), HALF:] = part_z[s, zi(3), HALF:] + rz0[s, 1]
            z1(s, 3).start()

        def second_x(s):
            x1(s).wait_recv()
            part_x[s, x] = part_x[s, x] + rx1[s]
            for off in (2, 1, 3):
                x2(s, off).start()

        def second_z(s):
            for role in (2, 3):
                z1(s, role).wait_recv()
            part_z[s, z] = part_z[s, z] + rz1[s, 0] + rz1[s, 1]
            z2(s).start()

        second_x(0)
        second_z(0)
        second_x(1)
        second_z(1)
        second_z(2)
        second_x(2)

        for off in (1, 2, 3):
            s3(off, zi(off)).wait_recv()
        sums = s3b[0] + s3b[1] + s3b[2] + s3b[3]
        sca[0] = sums[0]
        ratio = sums[0] / jnp.where(k > 1, sca[1], 1.0)
        beta = jnp.where(k == 0, 1.0, jnp.where(k == 1, 0.0, ratio))
        beta_row = beta[0:1, 0:1]
        sca[2] = sums[0] + 2.0 * beta * sums[1] + beta * beta * sca[2]

        def x3(s, off, peer):
            block = gx.at[s, x, peer]
            return remote(block, block, S_X3 + 3 * s + off - 1, R_X3 + N_Z * s + peer, zn(off))

        def x4(s, half, peer):
            block = gx.at[s, half, peer]
            i = N_Z * s + peer
            return remote(block, block, S_X4 + i, R_X4 + i, xn)

        def z4(s, role, incoming=False):
            if incoming:
                block = (
                    gz.at[s, zi(3)],
                    gz.at[s, zi(1)],
                    gz.at[s, zi(2), upper],
                    gz.at[s, zi(2), lower],
                )[role]
            else:
                block = (
                    gz.at[s, z],
                    gz.at[s, z],
                    gz.at[s, zi(3), upper],
                    gz.at[s, zi(1), lower],
                )[role]
            i = 4 * s + role
            return remote(block, block, S_Z4 + i, R_Z4 + i, zn(1 if role % 2 == 0 else 3))

        def own_x(s):
            for off in (1, 2, 3):
                x2(s, off).wait_recv()
            block = part_x[s, x, z] + rx2[s, 0] + rx2[s, 1] + rx2[s, 2]
            block = block * mask_x + beta_row * cprev_x[s]
            cprev_x[s] = block
            gx[s, x, z] = block
            for off in (2, 1, 3):
                x3(s, off, z).start()
            x4(s, x, z).start()

        def own_z(s):
            z2(s).wait_recv()
            block = part_z[s, z] + rz2[s]
            block = block * mask_z + beta_row * cprev_z[s]
            cprev_z[s] = block
            gz[s, z] = block
            z4(s, 0).start()
            z4(s, 1).start()

        def pass_x(s):
            for off in (1, 3, 2):
                x3(s, off, zi(off)).wait_recv()
                x4(s, x, zi(off)).start()

        def pass_z(s):
            for role in range(2):
                z4(s, role, True).wait_recv()
                z4(s, role + 2).start()

        own_x(0)
        own_x(1)
        own_z(0)
        own_x(2)
        own_z(1)
        own_z(2)
        pass_x(0)
        pass_x(1)
        pass_z(0)
        pass_x(2)
        pass_z(1)
        pass_z(2)
        state[1] = state[0] + beta_row * state[1]

        squares[...] = jnp.zeros_like(squares)
        for s in range(STAGES):
            for off in (0, 1, 3, 2):
                x4(s, 1 - x, zi(off)).wait_recv()
                if off == 2:
                    z4(s, 2, True).wait_recv()
                    z4(s, 3, True).wait_recv()
                left = jnp.concatenate([gx[s, 0, zi(off)], gx[s, 1, zi(off)]], axis=0)
                both = jnp.concatenate([left, gz[s, zi(off)]], axis=1)
                product = dot_t(both.astype(BF16), wb[s * N_Z + zi(off)])
                if s == 0 and off == 0:
                    cot[...] = product
                else:
                    cot[...] = cot[...] + product
                squares[...] = squares[...] + both * both

        e2 = remote(cot.at[:, pl.ds(COLS, COLS)], e2r, S_E2, R_E2, sib)
        e2.start()
        sca[3] = jnp.broadcast_to(total(squares[...]), (8, 128))
        s6 = remote(sca.at[3], s6r, S_S6, R_S6, sib)
        s6.start()
        s6.wait_recv()

        parity = lax.rem(k, 2)

        def ar(i, side, peer):
            block = arb.at[parity, peer, side]
            r = R_AR + (parity * N_DP + peer) * 2 + side
            return remote(block, block, S_AR + 2 * i + side, r, (dpn(PEERS[i]), t))

        def sq(i, peer):
            block = sqb.at[parity, peer]
            r = R_SQ + parity * N_DP + peer
            return remote(block, block, S_SQ + i, r, (dpn(PEERS[i]), t))

        sqb[parity, d] = sca[3] + s6r[...]
        for i in range(N_DP - 1):
            sq(i, d).start()
        e2.wait_recv()
        def gradient(side, cotangents):
            both = dot(ut[side], jnp.concatenate(cotangents, axis=1))
            arb[parity, d, side] = ADAPTER_SCALE * (both[:RANK] + both[RANK:])
            for i in range(N_DP - 1):
                ar(i, side, d).start()

        cotan = (cot[:, :COLS] + e2r[...]).astype(BF16)
        cotan = [cotan[:, h * HEAD_DIM : (h + 1) * HEAD_DIM] for h in range(HEADS)]
        gradient(1, [dot(pbt[h], a).astype(BF16) for h, a in enumerate(cotan)])
        dprobs = [dot_t(a, v_ref[:, n]) for a, n in zip(cotan, lanes)]
        tilted = [pf[h] * a for h, a in enumerate(dprobs)]
        dscores = [
            ((a - pf[h] * jnp.sum(a, axis=-1, keepdims=True)) * HEAD_DIM ** (-0.5)).astype(BF16)
            for h, a in enumerate(tilted)
        ]
        gradient(0, [dot(a, k_ref[:, n]).astype(BF16) for a, n in zip(dscores, lanes)])

        e1.wait_send()
        s1.wait_send()
        s2.wait_send()
        for off in (1, 2, 3):
            s3(off, z).wait_send()
        for s in range(STAGES):
            x1(s).wait_send()
            z2(s).wait_send()
            for off in (1, 2, 3):
                x2(s, off).wait_send()
                x3(s, off, z).wait_send()
            for peer in range(N_Z):
                x4(s, x, peer).wait_send()
                z4(s, peer).wait_send()
            for role in range(4):
                z1(s, role).wait_send()
        e2.wait_send()
        s6.wait_send()

        for i in reversed(range(N_DP - 1)):
            sq(i, dpn(PEERS[i])).wait_recv()
            for side in range(2):
                ar(i, side, dpn(PEERS[i])).wait_recv()
        for i in range(N_DP - 1):
            sq(i, d).wait_send()
            for side in range(2):
                ar(i, side, d).wait_send()
        summed = [arb[parity, 0, side] for side in range(2)]
        for peer in range(1, N_DP):
            summed = [a + arb[parity, peer, side] for side, a in enumerate(summed)]
        summed = jnp.concatenate(summed, axis=0)
        image = summed * (1.0 / (ROWS * N_DP)) + DAMP * state[1]
        squared = sqb[parity, 0]
        for peer in range(1, N_DP):
            squared = squared + sqb[parity, peer]
        squared = squared * (1.0 / (ROWS * N_DP))
        curvature = squared + DAMP * sca[2]
        alpha = jnp.where(k == 0, 1.0, sca[0] / jnp.where(k == 0, 1.0, curvature))[0:1, 0:1]
        state[2] = state[2] + jnp.where(k == 0, 0.0, alpha) * state[1]
        state[0] = state[0] - alpha * image
        sca[1] = sca[0]

    for j in range(CHUNKS):
        w_copy(j).wait_send()
    step_ref[...] = state[2]
    remain_ref[...] = state[0]


def solve(lengths, gain, bias, bq, bv, inputs, targets, wq, wk, wv, dq, dv, w_out):
    vmem = pl.BlockSpec(memory_space=pltpu.VMEM)
    square = (HEADS, HEAD_DIM, HEAD_DIM)
    half_block = (HALF, LANES)
    block = (ROWS, LANES)
    scratch = [
        pltpu.VMEM((ROWS, WIDTH), BF16),
        pltpu.VMEM((STAGES,) + half_block, BF16),
        pltpu.VMEM((STAGES,) + block, BF16),
        pltpu.VMEM((ROWS, WIDTH), BF16),
        pltpu.VMEM((WIDTH, 3 * COLS), BF16),
        pltpu.VMEM((ROWS, 3 * COLS), F32),
        pltpu.VMEM((2 * RANK, WIDTH), BF16),
        pltpu.VMEM((ROWS, COLS), BF16),
        pltpu.VMEM((ROWS, COLS), BF16),
        pltpu.VMEM((ROWS, COLS), BF16),
        pltpu.VMEM((CHUNKS, 2 * COLS, PAIR), BF16),
        pltpu.VMEM((CHUNKS, COLS, PAIR), BF16),
        pltpu.VMEM((CHUNKS, COLS, PAIR), F32),
        pltpu.VMEM((CHUNKS, COLS, PAIR), F32),
        pltpu.VMEM(square, F32),
        pltpu.VMEM(square, BF16),
        pltpu.VMEM(square, BF16),
        pltpu.VMEM((2, ROWS, 3 * RANK), BF16),
        pltpu.VMEM((2, 2 * RANK, ROWS), BF16),
        pltpu.VMEM((ROWS, 2 * COLS), BF16),
        pltpu.VMEM((STAGES, N_Z, ROWS, PAIR), F32),
        pltpu.VMEM((ROWS, COLS), F32),
        pltpu.VMEM((ROWS, COLS), F32),
        pltpu.VMEM((STAGES, 2, N_Z) + half_block, F32),
        pltpu.VMEM((STAGES, N_Z) + block, F32),
        pltpu.VMEM((STAGES, N_Z) + half_block, F32),
        pltpu.VMEM((STAGES, 2) + half_block, F32),
        pltpu.VMEM((STAGES, 2) + block, F32),
        pltpu.VMEM((STAGES, N_Z - 1) + half_block, F32),
        pltpu.VMEM((STAGES,) + block, F32),
        pltpu.VMEM((STAGES, 2, N_Z) + half_block, F32),
        pltpu.VMEM((STAGES, N_Z) + block, F32),
        pltpu.VMEM((STAGES,) + half_block, F32),
        pltpu.VMEM((STAGES,) + block, F32),
        pltpu.VMEM((ROWS, 2 * COLS), F32),
        pltpu.VMEM((ROWS, COLS), F32),
        pltpu.VMEM((2, N_DP, 2, RANK, COLS), F32),
        pltpu.VMEM((2, N_DP, 8, 128), F32),
        pltpu.VMEM((ROWS, PAIR), F32),
        pltpu.VMEM((3, 2 * RANK, COLS), F32),
        pltpu.VMEM((8, 8, 128), F32),
        pltpu.VMEM((2, 8, 128), F32),
        pltpu.VMEM((2, 8, 128), F32),
        pltpu.VMEM((N_Z, 2, 8, 128), F32),
        pltpu.VMEM((8, 128), F32),
        pltpu.SemaphoreType.DMA((2 * CHUNKS,)),
        pltpu.SemaphoreType.DMA((36,)),
        pltpu.SemaphoreType.DMA((N_SEND,)),
        pltpu.SemaphoreType.DMA((N_RECV,)),
    ]
    shape = jax.ShapeDtypeStruct((2 * RANK, COLS), F32)
    return pl.pallas_call(
        kernel,
        out_shape=(shape, shape),
        in_specs=[pl.BlockSpec(memory_space=pltpu.SMEM)]
        + [vmem] * 4
        + [pl.BlockSpec(memory_space=pl.ANY)] * 8,
        out_specs=(vmem, vmem),
        scratch_shapes=scratch,
        compiler_params=pltpu.CompilerParams(
            collective_id=0, has_side_effects=True, vmem_limit_bytes=58 * 2**20
        ),
        cost_estimate=pl.CostEstimate(
            flops=8 * 2 * ROWS * WIDTH * COLS, bytes_accessed=8 * 2**20, transcendentals=0
        ),
        name="newton",
    )(lengths, gain, bias, bq, bv, inputs, targets, wq, wk, wv, dq, dv, w_out)


def on_device(
    inputs,
    targets,
    lengths,
    ln_gain,
    ln_bias,
    query_weight,
    w_key,
    value_weight,
    w_out,
    down_query,
    down_value,
    query_up_factor,
    value_up_factor,
):
    step, remain = solve(
        lengths,
        ln_gain.reshape(1, WIDTH),
        ln_bias.reshape(1, WIDTH),
        query_up_factor,
        value_up_factor,
        inputs,
        targets,
        query_weight,
        w_key,
        value_weight,
        down_query.T,
        down_value.T,
        w_out,
    )
    return (step[:RANK], step[RANK:], remain[:RANK], remain[RANK:])


def solution(mesh):
    in_specs = (
        P("dp", None),
        P("dp", None),
        P("dp"),
        P(),
        P(),
        P(None, "tensor"),
        P(None, "tensor"),
        P(None, "tensor"),
        P("tensor", None),
        P(),
        P(),
        P(None, "tensor"),
        P(None, "tensor"),
    )
    out_specs = (P(None, "tensor"), P(None, "tensor"), P(None, "tensor"), P(None, "tensor"))
    return jax.shard_map(
        on_device, mesh=mesh, in_specs=in_specs, out_specs=out_specs, check_vma=False
    )
```

```python
import jax
import jax.numpy as jnp
from jax import lax
from jax.experimental import pallas as pl
from jax.experimental.pallas import tpu as pltpu
from jax.sharding import PartitionSpec as P

HEAD_DIM = 128
CG_STEPS = 3
HEADS = 3
COLS = HEADS * HEAD_DIM
ROWS = 128
HALF = ROWS // 2
RANK = 16
WIDTH = 6144
CORE_WIDTH = WIDTH // 2
STAGES = 3
LANES = 128
PAIR = 2 * LANES
CHUNKS = CORE_WIDTH // PAIR
N_DP = 8
N_Z = 4
DEPTH = 768

EPS = 1e-05
ADAPTER_SCALE = 2.0
DAMP = 0.05
NEG = -1e30

F32 = jnp.float32
BF16 = jnp.bfloat16
MESH = pl.DeviceIdType.MESH

S_W, S_E1, S_S1, S_S2, S_S3, S_S6, S_E2, S_X1, S_Z1, S_X2 = 0, 12, 15, 16, 17, 20, 21, 22, 34, 46
S_Z2, S_X3, S_X4, S_Z4, S_AR, S_SQ, N_SEND = 55, 58, 67, 79, 91, 105, 112
R_W, R_E1, R_S1, R_S2, R_S3, R_S6, R_E2, R_X1, R_Z1, R_X2 = 0, 12, 15, 16, 17, 21, 22, 23, 35, 47
R_Z2, R_X3, R_X4, R_Z4, R_AR, R_SQ, N_RECV = 56, 59, 71, 83, 95, 127, 143

PEERS = ((1, 2), (1, 1), (1, 3), (0, 2), (1, 0), (0, 1), (0, 3))


def dot(a, b):
    return lax.dot_general(a, b, (((1,), (0,)), ((), ())), preferred_element_type=F32)


def dot_t(a, b):
    return lax.dot_general(a, b, (((1,), (1,)), ((), ())), preferred_element_type=F32)


def split_high_low(x):
    high = x.astype(BF16)
    return high, (x - high.astype(F32)).astype(BF16)


def total(x):
    return jnp.sum(jnp.sum(x, axis=1, keepdims=True), axis=0, keepdims=True)


def kernel(
    len_ref,
    gain_ref,
    bias_ref,
    bq_ref,
    bv_ref,
    inputs_ref,
    targets_ref,
    wq_ref,
    wk_ref,
    wv_ref,
    dq_ref,
    dv_ref,
    w_ref,
    step_ref,
    remain_ref,
    inputs_v,
    targets_x,
    targets_z,
    normed,
    weights_v,
    rows_v,
    down_v,
    q_ref,
    k_ref,
    v_ref,
    wb,
    wtmp,
    wsend,
    wrecv,
    pf,
    pb,
    pbt,
    u3,
    ut,
    dmcat,
    begun,
    e1s,
    e1r,
    part_x,
    part_z,
    rx1,
    rz0,
    rz1,
    rx2,
    rz2,
    gx,
    gz,
    cprev_x,
    cprev_z,
    cot,
    e2r,
    arb,
    sqb,
    squares,
    state,
    sca,
    s1r,
    s2r,
    s3b,
    s6r,
    lsem,
    psem,
    ssem,
    rsem,
):
    d = lax.axis_index("dp")
    t = lax.axis_index("tensor")
    c = lax.rem(t, 2)
    x = lax.rem(t // 2, 2)
    z = t // 4
    sib = (d, t + 1 - 2 * c)
    xn = (d, t + 2 - 4 * x)

    def zn(off):
        return (d, lax.rem(t + 4 * off, 16))

    def dpn(hop):
        return lax.rem(d // 4 + hop[0], 2) * 4 + lax.rem(d + hop[1], 4)

    def remote(src, dst, s, r, device):
        return pltpu.make_async_remote_copy(
            src_ref=src,
            dst_ref=dst,
            send_sem=ssem.at[s],
            recv_sem=rsem.at[r],
            device_id=device,
            device_id_type=MESH,
        )

    barrier = pltpu.get_barrier_semaphore()
    partners = [sib, xn] + [zn(o) for o in (1, 2, 3)] + [(dpn(hop), t) for hop in PEERS]
    for device in partners:
        pl.semaphore_signal(barrier, inc=1, device_id=device, device_id_type=MESH)

    def own_copy(j):
        columns = pl.ds(pl.multiple_of(c * CORE_WIDTH + j * PAIR, PAIR), PAIR)
        return pltpu.make_async_copy(
            w_ref.at[:, columns], wb.at[j, pl.ds(0, COLS)], lsem.at[j]
        )

    def other_copy(j):
        columns = pl.ds(pl.multiple_of((1 - c) * CORE_WIDTH + j * PAIR, PAIR), PAIR)
        return pltpu.make_async_copy(w_ref.at[:, columns], wtmp.at[j], lsem.at[CHUNKS + j])

    def w_copy(j):
        return remote(wsend.at[j], wrecv.at[j], S_W + j, R_W + j, sib)

    def order(i):
        return i // N_Z * N_Z + lax.rem(z + lax.rem(i + 2, N_Z), N_Z)

    def load(source, target, pieces, first):
        rows = source.shape[0] // pieces
        return [
            pltpu.make_async_copy(
                source.at[pl.ds(i * rows, rows)], target.at[pl.ds(i * rows, rows)], psem.at[first + i]
            )
            for i in range(pieces)
        ]

    load_inputs = load(inputs_ref, inputs_v, 4, 0)
    load_downs = [
        pltpu.make_async_copy(ref, down_v.at[pl.ds(i * RANK, RANK)], psem.at[4 + i])
        for i, ref in enumerate((dq_ref, dv_ref))
    ]
    half_rows = pl.ds(pl.multiple_of(x * HALF, HALF), HALF)

    def gap_lanes(s, region):
        left = c * CORE_WIDTH + (s * N_Z + z) * PAIR + region * LANES
        return pl.ds(pl.multiple_of(left, LANES), LANES)

    load_targets = []
    for s in range(STAGES):
        for i, (rows, target) in enumerate(((half_rows, targets_x), (pl.ds(0, ROWS), targets_z))):
            source = targets_ref.at[rows, gap_lanes(s, i)]
            load_targets.append(
                pltpu.make_async_copy(source, target.at[s], psem.at[6 + 2 * s + i])
            )

    def load_weights(i):
        rows = pl.ds(i * DEPTH, DEPTH)
        return [
            pltpu.make_async_copy(
                ref.at[rows],
                weights_v.at[rows, pl.ds(n * COLS, COLS)],
                psem.at[12 + 3 * i + n],
            )
            for n, ref in enumerate((wq_ref, wk_ref, wv_ref))
        ]

    pieces = [load_weights(i) for i in range(WIDTH // DEPTH)]
    for copy in load_inputs:
        copy.start()

    @pl.loop(0, CHUNKS)
    def _(i):
        other_copy(order(i)).start()

    for copy in load_downs + sum(pieces[:4], []):
        copy.start()

    for i, copy in enumerate(load_inputs):
        copy.wait()
        if i < 2:
            for late in pieces[4 + 2 * i] + pieces[5 + 2 * i]:
                late.start()
        if i == 2:

            @pl.loop(0, CHUNKS)
            def _(j):
                own_copy(order(j)).start()

            for late in load_targets:
                late.start()

        if i == 1:
            pl.semaphore_wait(barrier, len(partners))
        if i:

            @pl.loop(4 * (i - 1), 4 * i)
            def _(n):
                j = order(n)
                other_copy(j).wait()
                wsend[j] = wtmp[j].astype(F32)
                w_copy(j).start()

        size = ROWS // len(load_inputs)

        @pl.loop(i * size // 16, (i + 1) * size // 16)
        def _(r):
            rows = pl.ds(pl.multiple_of(r * 16, 16), 16)
            wide = inputs_v[rows, :].astype(F32)
            centred = wide - jnp.sum(wide, axis=1, keepdims=True) * (1.0 / WIDTH)
            spread = jnp.sum(centred * centred, axis=1, keepdims=True) * (1.0 / WIDTH)
            scaled = centred * lax.rsqrt(spread + EPS)
            normed[rows, :] = (scaled * gain_ref[...] + bias_ref[...]).astype(BF16)

    for i, piece in enumerate(pieces):
        for copy in piece:
            copy.wait()
        depth = pl.ds(i * DEPTH, DEPTH)
        product = dot(normed[:, depth], weights_v[depth, :])
        rows_v[...] = product if i == 0 else rows_v[...] + product
    for copy in load_downs:
        copy.wait()
    lows = dot_t(normed[...], down_v[...])
    lows_t = lows.T
    k_ref[...] = rows_v[:, COLS : 2 * COLS].astype(BF16)
    for i, (target, up) in enumerate(((q_ref, bq_ref), (v_ref, bv_ref))):
        ranks = slice(i * RANK, (i + 1) * RANK)
        high, rest = split_high_low(lows[:, ranks])
        u3[i] = jnp.concatenate([high, high, rest], axis=1)
        high, rest = split_high_low(lows_t[ranks])
        ut[i] = jnp.concatenate([high, rest], axis=0)
        high, rest = split_high_low(up[...])
        stacked = jnp.concatenate([high, rest, high], axis=0)
        rows = rows_v[:, 2 * i * COLS : (2 * i + 1) * COLS]
        target[...] = (rows + ADAPTER_SCALE * dot(u3[i], stacked)).astype(BF16)

    limit = len_ref[0]
    row = lax.broadcasted_iota(jnp.int32, (ROWS, ROWS), 0)
    col = lax.broadcasted_iota(jnp.int32, (ROWS, ROWS), 1)
    live = (col <= row) & (col < limit)
    lanes = [pl.ds(h * HEAD_DIM, HEAD_DIM) for h in range(HEADS)]
    scores = [dot_t(q_ref[:, n], k_ref[:, n]) * HEAD_DIM ** (-0.5) for n in lanes]
    scores = [jnp.where(live, a, NEG) for a in scores]
    weights = [jnp.exp(a - jnp.max(a, axis=-1, keepdims=True)) for a in scores]
    probs = [a / jnp.sum(a, axis=-1, keepdims=True) for a in weights]
    mixed = [dot(a.astype(BF16), v_ref[:, n]).astype(BF16) for a, n in zip(probs, lanes)]
    for h, n in enumerate(lanes):
        pf[h] = probs[h]
        pb[h] = probs[h].astype(BF16)
        pbt[h] = probs[h].T.astype(BF16)
        dmcat[:, n] = mixed[h]
        e1s[:, n] = mixed[h].astype(F32)
    place = lax.broadcasted_iota(jnp.int32, (ROWS, LANES), 0)
    mask_z = (place < limit).astype(F32)
    mask_x = (place[:HALF] + x * HALF < limit).astype(F32)
    for copy in load_targets:
        copy.wait()
    for s in range(STAGES):
        gap = inputs_v[half_rows, gap_lanes(s, 0)].astype(F32) - targets_x[s].astype(F32)
        cprev_x[s] = gap * mask_x
        gap = inputs_v[:, gap_lanes(s, 1)].astype(F32) - targets_z[s].astype(F32)
        cprev_z[s] = gap * mask_z
    state[...] = jnp.zeros_like(state)
    sca[...] = jnp.zeros_like(sca)

    @pl.loop(0, CG_STEPS + 1)
    def _(k):
        @pl.when(k > 0)
        def _():
            tangents = []
            for i in range(2):
                high, low = split_high_low(state[0, i * RANK : (i + 1) * RANK])
                stacked = jnp.concatenate([high, low, high], axis=0)
                tangents.append((ADAPTER_SCALE * dot(u3[i], stacked)).astype(BF16))
            dq, dv = [[a[:, h * HEAD_DIM : (h + 1) * HEAD_DIM] for h in range(HEADS)] for a in tangents]
            scores = [dot_t(a, k_ref[:, n]) * HEAD_DIM ** (-0.5) for a, n in zip(dq, lanes)]
            tilted = [pf[h] * a for h, a in enumerate(scores)]
            dprobs = [
                (a - pf[h] * jnp.sum(a, axis=-1, keepdims=True)).astype(BF16)
                for h, a in enumerate(tilted)
            ]
            left = [jnp.concatenate([a, pb[h]], axis=1) for h, a in enumerate(dprobs)]
            right = [jnp.concatenate([v_ref[:, n], a], axis=0) for a, n in zip(dv, lanes)]
            dmixed = [dot(a, b).astype(BF16) for a, b in zip(left, right)]
            for a, n in zip(dmixed, lanes):
                e1s[:, n] = a.astype(F32)
                dmcat[:, n] = a

        e1 = remote(e1s, e1r, S_E1, R_E1, sib)
        e1.start()
        sca[4] = jnp.broadcast_to(total(state[0] * state[0]), (8, 128))
        sca[5] = jnp.broadcast_to(total(state[0] * state[1]), (8, 128))
        s1 = remote(sca.at[pl.ds(4, 2)], s1r, S_S1, R_S1, sib)
        s1.start()
        @pl.when(k == 0)
        def _():
            for j in range(CHUNKS):
                own_copy(j).wait()

        for s in range(STAGES):
            for off in (2, 1, 3, 0):
                begun[s, off] = dot(dmcat[:, :PAIR], wb[s * N_Z + lax.rem(z + off, N_Z), :PAIR])
        e1.wait_recv()
        dmcat[:, pl.ds(COLS, COLS)] = e1r[...].astype(BF16)
        s1.wait_recv()
        sca[pl.ds(6, 2)] = sca[pl.ds(4, 2)] + s1r[...]
        s2 = remote(sca.at[pl.ds(6, 2)], s2r, S_S2, R_S2, xn)
        s2.start()

        def zi(off):
            return lax.rem(z + off, N_Z)

        def x1(s, off):
            i = N_Z * s + off
            source, target = part_x.at[s, 1 - x, zi(off)], rx1.at[s, zi(off)]
            return remote(source, target, S_X1 + i, R_X1 + i, xn)

        upper, lower = pl.ds(0, HALF), pl.ds(HALF, HALF)

        def z1(s, role):
            to, row, target = (
                (2, upper, rz0.at[s, 0]),
                (2, lower, rz0.at[s, 1]),
                (1, pl.ds(0, ROWS), rz1.at[s, 0]),
                (3, pl.ds(0, ROWS), rz1.at[s, 1]),
            )[role]
            i = 4 * s + role
            source = part_z.at[s, zi(to), row]
            return remote(source, target, S_Z1 + i, R_Z1 + i, zn(1 if role % 2 == 0 else 3))

        def x2(s, off):
            i = 3 * s + off - 1
            return remote(part_x.at[s, x, zi(off)], rx2.at[s, off - 1], S_X2 + i, R_X2 + i, zn(off))

        def z2(s):
            return remote(part_z.at[s, z], rz2.at[s], S_Z2 + s, R_Z2 + s, xn)

        for s in range(STAGES):

            @pl.when(k == 0)
            def _():
                for off in (2, 3, 0, 1):
                    j = s * N_Z + zi(off)
                    w_copy(j).wait_recv()
                    wb[j, pl.ds(COLS, COLS)] = wrecv[j].astype(BF16)

            for off in (2, 1, 3, 0):
                product = begun[s, off] + dot(dmcat[:, PAIR:], wb[s * N_Z + zi(off), PAIR:])
                part_z[s, zi(off)] = product[:, LANES:]
                for role in (0, 1) if off == 2 else ():
                    z1(s, role).start()
                part_x[s, 0, zi(off)] = product[:HALF, :LANES]
                part_x[s, 1, zi(off)] = product[HALF:, :LANES]
                x1(s, off).start()

        s2.wait_recv()
        s3b[z] = sca[pl.ds(6, 2)] + s2r[...]

        def s3(off, peer):
            return remote(s3b.at[peer], s3b.at[peer], S_S3 + off - 1, R_S3 + peer, zn(off))

        for off in (2, 1, 3):
            s3(off, z).start()

        for s in range(STAGES):
            z1(s, 0).wait_recv()
            part_z[s, zi(1), :HALF] = part_z[s, zi(1), :HALF] + rz0[s, 0]
            z1(s, 2).start()
            z1(s, 1).wait_recv()
            part_z[s, zi(3), HALF:] = part_z[s, zi(3), HALF:] + rz0[s, 1]
            z1(s, 3).start()

        def second_x(s):
            for off in (2, 1, 3, 0):
                x1(s, off).wait_recv()
                part_x[s, x, zi(off)] = part_x[s, x, zi(off)] + rx1[s, zi(off)]
                if off:
                    x2(s, off).start()

        def second_z(s):
            for role in (2, 3):
                z1(s, role).wait_recv()
            part_z[s, z] = part_z[s, z] + rz1[s, 0] + rz1[s, 1]
            z2(s).start()

        second_x(0)
        second_z(0)
        second_x(1)
        second_z(1)
        second_z(2)
        second_x(2)

        for off in (1, 2, 3):
            s3(off, zi(off)).wait_recv()
        sums = s3b[0] + s3b[1] + s3b[2] + s3b[3]
        sca[0] = sums[0]
        ratio = sums[0] / jnp.where(k > 1, sca[1], 1.0)
        beta = jnp.where(k == 0, 1.0, jnp.where(k == 1, 0.0, ratio))
        beta_row = beta[0:1, 0:1]
        sca[2] = sums[0] + 2.0 * beta * sums[1] + beta * beta * sca[2]

        def x3(s, off, peer):
            block = gx.at[s, x, peer]
            return remote(block, block, S_X3 + 3 * s + off - 1, R_X3 + N_Z * s + peer, zn(off))

        def x4(s, half, peer):
            block = gx.at[s, half, peer]
            i = N_Z * s + peer
            return remote(block, block, S_X4 + i, R_X4 + i, xn)

        def z4(s, role, incoming=False):
            if incoming:
                block = (
                    gz.at[s, zi(3)],
                    gz.at[s, zi(1)],
                    gz.at[s, zi(2), upper],
                    gz.at[s, zi(2), lower],
                )[role]
            else:
                block = (
                    gz.at[s, z],
                    gz.at[s, z],
                    gz.at[s, zi(3), upper],
                    gz.at[s, zi(1), lower],
                )[role]
            i = 4 * s + role
            return remote(block, block, S_Z4 + i, R_Z4 + i, zn(1 if role % 2 == 0 else 3))

        def own_x(s):
            for off in (1, 2, 3):
                x2(s, off).wait_recv()
            block = part_x[s, x, z] + rx2[s, 0] + rx2[s, 1] + rx2[s, 2]
            block = block * mask_x + beta_row * cprev_x[s]
            cprev_x[s] = block
            gx[s, x, z] = block
            for off in (2, 1, 3):
                x3(s, off, z).start()
            x4(s, x, z).start()

        def own_z(s):
            z2(s).wait_recv()
            block = part_z[s, z] + rz2[s]
            block = block * mask_z + beta_row * cprev_z[s]
            cprev_z[s] = block
            gz[s, z] = block
            z4(s, 0).start()
            z4(s, 1).start()

        def pass_x(s):
            for off in (1, 3, 2):
                x3(s, off, zi(off)).wait_recv()
                x4(s, x, zi(off)).start()

        def pass_z(s):
            for role in range(2):
                z4(s, role, True).wait_recv()
                z4(s, role + 2).start()

        own_x(0)
        own_x(1)
        own_z(0)
        own_x(2)
        own_z(1)
        own_z(2)
        pass_x(0)
        pass_x(1)
        pass_z(0)
        pass_x(2)
        pass_z(1)
        pass_z(2)
        state[1] = state[0] + beta_row * state[1]

        squares[...] = jnp.zeros_like(squares)
        for s in range(STAGES):
            for off in (0, 1, 3, 2):
                x4(s, 1 - x, zi(off)).wait_recv()
                if off == 2:
                    z4(s, 2, True).wait_recv()
                    z4(s, 3, True).wait_recv()
                left = jnp.concatenate([gx[s, 0, zi(off)], gx[s, 1, zi(off)]], axis=0)
                both = jnp.concatenate([left, gz[s, zi(off)]], axis=1)
                product = dot_t(both.astype(BF16), wb[s * N_Z + zi(off)])
                if s == 0 and off == 0:
                    cot[...] = product
                else:
                    cot[...] = cot[...] + product
                squares[...] = squares[...] + both * both

        e2 = remote(cot.at[:, pl.ds(COLS, COLS)], e2r, S_E2, R_E2, sib)
        e2.start()
        sca[3] = jnp.broadcast_to(total(squares[...]), (8, 128))
        s6 = remote(sca.at[3], s6r, S_S6, R_S6, sib)
        s6.start()
        s6.wait_recv()

        parity = lax.rem(k, 2)

        def ar(i, side, peer):
            block = arb.at[parity, peer, side]
            r = R_AR + (parity * N_DP + peer) * 2 + side
            return remote(block, block, S_AR + 2 * i + side, r, (dpn(PEERS[i]), t))

        def sq(i, peer):
            block = sqb.at[parity, peer]
            r = R_SQ + parity * N_DP + peer
            return remote(block, block, S_SQ + i, r, (dpn(PEERS[i]), t))

        sqb[parity, d] = sca[3] + s6r[...]
        for i in range(N_DP - 1):
            sq(i, d).start()
        e2.wait_recv()
        def gradient(side, cotangents):
            both = dot(ut[side], jnp.concatenate(cotangents, axis=1))
            arb[parity, d, side] = ADAPTER_SCALE * (both[:RANK] + both[RANK:])
            for i in range(N_DP - 1):
                ar(i, side, d).start()

        cotan = (cot[:, :COLS] + e2r[...]).astype(BF16)
        cotan = [cotan[:, h * HEAD_DIM : (h + 1) * HEAD_DIM] for h in range(HEADS)]
        gradient(1, [dot(pbt[h], a).astype(BF16) for h, a in enumerate(cotan)])
        dprobs = [dot_t(a, v_ref[:, n]) for a, n in zip(cotan, lanes)]
        tilted = [pf[h] * a for h, a in enumerate(dprobs)]
        dscores = [
            ((a - pf[h] * jnp.sum(a, axis=-1, keepdims=True)) * HEAD_DIM ** (-0.5)).astype(BF16)
            for h, a in enumerate(tilted)
        ]
        gradient(0, [dot(a, k_ref[:, n]).astype(BF16) for a, n in zip(dscores, lanes)])

        e1.wait_send()
        s1.wait_send()
        s2.wait_send()
        for off in (1, 2, 3):
            s3(off, z).wait_send()
        for s in range(STAGES):
            for off in range(N_Z):
                x1(s, off).wait_send()
            z2(s).wait_send()
            for off in (1, 2, 3):
                x2(s, off).wait_send()
                x3(s, off, z).wait_send()
            for peer in range(N_Z):
                x4(s, x, peer).wait_send()
                z4(s, peer).wait_send()
            for role in range(4):
                z1(s, role).wait_send()
        e2.wait_send()
        s6.wait_send()

        for i in reversed(range(N_DP - 1)):
            sq(i, dpn(PEERS[i])).wait_recv()
            for side in range(2):
                ar(i, side, dpn(PEERS[i])).wait_recv()
        for i in range(N_DP - 1):
            sq(i, d).wait_send()
            for side in range(2):
                ar(i, side, d).wait_send()
        summed = [arb[parity, 0, side] for side in range(2)]
        for peer in range(1, N_DP):
            summed = [a + arb[parity, peer, side] for side, a in enumerate(summed)]
        summed = jnp.concatenate(summed, axis=0)
        image = summed * (1.0 / (ROWS * N_DP)) + DAMP * state[1]
        squared = sqb[parity, 0]
        for peer in range(1, N_DP):
            squared = squared + sqb[parity, peer]
        squared = squared * (1.0 / (ROWS * N_DP))
        curvature = squared + DAMP * sca[2]
        alpha = jnp.where(k == 0, 1.0, sca[0] / jnp.where(k == 0, 1.0, curvature))[0:1, 0:1]
        state[2] = state[2] + jnp.where(k == 0, 0.0, alpha) * state[1]
        state[0] = state[0] - alpha * image
        sca[1] = sca[0]

    for j in range(CHUNKS):
        w_copy(j).wait_send()
    step_ref[...] = state[2]
    remain_ref[...] = state[0]


def solve(lengths, gain, bias, bq, bv, inputs, targets, wq, wk, wv, dq, dv, w_out):
    vmem = pl.BlockSpec(memory_space=pltpu.VMEM)
    square = (HEADS, HEAD_DIM, HEAD_DIM)
    half_block = (HALF, LANES)
    block = (ROWS, LANES)
    scratch = [
        pltpu.VMEM((ROWS, WIDTH), BF16),
        pltpu.VMEM((STAGES,) + half_block, BF16),
        pltpu.VMEM((STAGES,) + block, BF16),
        pltpu.VMEM((ROWS, WIDTH), BF16),
        pltpu.VMEM((WIDTH, 3 * COLS), BF16),
        pltpu.VMEM((ROWS, 3 * COLS), F32),
        pltpu.VMEM((2 * RANK, WIDTH), BF16),
        pltpu.VMEM((ROWS, COLS), BF16),
        pltpu.VMEM((ROWS, COLS), BF16),
        pltpu.VMEM((ROWS, COLS), BF16),
        pltpu.VMEM((CHUNKS, 2 * COLS, PAIR), BF16),
        pltpu.VMEM((CHUNKS, COLS, PAIR), BF16),
        pltpu.VMEM((CHUNKS, COLS, PAIR), F32),
        pltpu.VMEM((CHUNKS, COLS, PAIR), F32),
        pltpu.VMEM(square, F32),
        pltpu.VMEM(square, BF16),
        pltpu.VMEM(square, BF16),
        pltpu.VMEM((2, ROWS, 3 * RANK), BF16),
        pltpu.VMEM((2, 2 * RANK, ROWS), BF16),
        pltpu.VMEM((ROWS, 2 * COLS), BF16),
        pltpu.VMEM((STAGES, N_Z, ROWS, PAIR), F32),
        pltpu.VMEM((ROWS, COLS), F32),
        pltpu.VMEM((ROWS, COLS), F32),
        pltpu.VMEM((STAGES, 2, N_Z) + half_block, F32),
        pltpu.VMEM((STAGES, N_Z) + block, F32),
        pltpu.VMEM((STAGES, N_Z) + half_block, F32),
        pltpu.VMEM((STAGES, 2) + half_block, F32),
        pltpu.VMEM((STAGES, 2) + block, F32),
        pltpu.VMEM((STAGES, N_Z - 1) + half_block, F32),
        pltpu.VMEM((STAGES,) + block, F32),
        pltpu.VMEM((STAGES, 2, N_Z) + half_block, F32),
        pltpu.VMEM((STAGES, N_Z) + block, F32),
        pltpu.VMEM((STAGES,) + half_block, F32),
        pltpu.VMEM((STAGES,) + block, F32),
        pltpu.VMEM((ROWS, 2 * COLS), F32),
        pltpu.VMEM((ROWS, COLS), F32),
        pltpu.VMEM((2, N_DP, 2, RANK, COLS), F32),
        pltpu.VMEM((2, N_DP, 8, 128), F32),
        pltpu.VMEM((ROWS, PAIR), F32),
        pltpu.VMEM((3, 2 * RANK, COLS), F32),
        pltpu.VMEM((8, 8, 128), F32),
        pltpu.VMEM((2, 8, 128), F32),
        pltpu.VMEM((2, 8, 128), F32),
        pltpu.VMEM((N_Z, 2, 8, 128), F32),
        pltpu.VMEM((8, 128), F32),
        pltpu.SemaphoreType.DMA((2 * CHUNKS,)),
        pltpu.SemaphoreType.DMA((36,)),
        pltpu.SemaphoreType.DMA((N_SEND,)),
        pltpu.SemaphoreType.DMA((N_RECV,)),
    ]
    shape = jax.ShapeDtypeStruct((2 * RANK, COLS), F32)
    return pl.pallas_call(
        kernel,
        out_shape=(shape, shape),
        in_specs=[pl.BlockSpec(memory_space=pltpu.SMEM)]
        + [vmem] * 4
        + [pl.BlockSpec(memory_space=pl.ANY)] * 8,
        out_specs=(vmem, vmem),
        scratch_shapes=scratch,
        compiler_params=pltpu.CompilerParams(
            collective_id=0, has_side_effects=True, vmem_limit_bytes=58 * 2**20
        ),
        cost_estimate=pl.CostEstimate(
            flops=8 * 2 * ROWS * WIDTH * COLS, bytes_accessed=8 * 2**20, transcendentals=0
        ),
        name="newton",
    )(lengths, gain, bias, bq, bv, inputs, targets, wq, wk, wv, dq, dv, w_out)


def on_device(
    inputs,
    targets,
    lengths,
    ln_gain,
    ln_bias,
    query_weight,
    w_key,
    value_weight,
    w_out,
    down_query,
    down_value,
    query_up_factor,
    value_up_factor,
):
    step, remain = solve(
        lengths,
        ln_gain.reshape(1, WIDTH),
        ln_bias.reshape(1, WIDTH),
        query_up_factor,
        value_up_factor,
        inputs,
        targets,
        query_weight,
        w_key,
        value_weight,
        down_query.T,
        down_value.T,
        w_out,
    )
    return (step[:RANK], step[RANK:], remain[:RANK], remain[RANK:])


def solution(mesh):
    in_specs = (
        P("dp", None),
        P("dp", None),
        P("dp"),
        P(),
        P(),
        P(None, "tensor"),
        P(None, "tensor"),
        P(None, "tensor"),
        P("tensor", None),
        P(),
        P(),
        P(None, "tensor"),
        P(None, "tensor"),
    )
    out_specs = (P(None, "tensor"), P(None, "tensor"), P(None, "tensor"), P(None, "tensor"))
    return jax.shard_map(
        on_device, mesh=mesh, in_specs=in_specs, out_specs=out_specs, check_vma=False
    )
```

```python
import jax
import jax.numpy as jnp
from jax import lax
from jax.experimental import pallas as pl
from jax.experimental.pallas import tpu as pltpu
from jax.sharding import PartitionSpec as P

HEAD_DIM = 128
CG_STEPS = 3
HEADS = 3
COLS = HEADS * HEAD_DIM
ROWS = 128
HALF = ROWS // 2
RANK = 16
WIDTH = 6144
CORE_WIDTH = WIDTH // 2
STAGES = 3
LANES = 128
PAIR = 2 * LANES
CHUNKS = CORE_WIDTH // PAIR
N_DP = 8
N_Z = 4
DEPTH = 768

EPS = 1e-05
ADAPTER_SCALE = 2.0
DAMP = 0.05
NEG = -1e30

F32 = jnp.float32
BF16 = jnp.bfloat16
MESH = pl.DeviceIdType.MESH

S_W, S_E1, S_S1, S_S2, S_S3, S_S6, S_E2, S_X1, S_Z1, S_X2 = 0, 12, 15, 16, 17, 20, 21, 22, 34, 46
S_Z2, S_X3, S_X4, S_Z4, S_AR, S_SQ, N_SEND = 55, 58, 67, 79, 91, 105, 112
R_W, R_E1, R_S1, R_S2, R_S3, R_S6, R_E2, R_X1, R_Z1, R_X2 = 0, 12, 15, 16, 17, 21, 22, 23, 35, 47
R_Z2, R_X3, R_X4, R_Z4, R_AR, R_SQ, N_RECV = 56, 59, 71, 83, 95, 127, 143

PEERS = ((1, 2), (1, 1), (1, 3), (0, 2), (1, 0), (0, 1), (0, 3))


def dot(a, b):
    return lax.dot_general(a, b, (((1,), (0,)), ((), ())), preferred_element_type=F32)


def dot_t(a, b):
    return lax.dot_general(a, b, (((1,), (1,)), ((), ())), preferred_element_type=F32)


def split_high_low(x):
    high = x.astype(BF16)
    return high, (x - high.astype(F32)).astype(BF16)


def total(x):
    return jnp.sum(jnp.sum(x, axis=1, keepdims=True), axis=0, keepdims=True)


def kernel(
    len_ref,
    gain_ref,
    bias_ref,
    bq_ref,
    bv_ref,
    inputs_ref,
    targets_ref,
    wq_ref,
    wk_ref,
    wv_ref,
    dq_ref,
    dv_ref,
    w_ref,
    step_ref,
    remain_ref,
    inputs_v,
    targets_x,
    targets_z,
    normed,
    weights_v,
    rows_v,
    down_v,
    q_ref,
    k_ref,
    v_ref,
    wb,
    wtmp,
    wsend,
    wrecv,
    pf,
    pb,
    pbt,
    u3,
    ut,
    dmcat,
    begun,
    e1s,
    e1r,
    part_x,
    part_z,
    rx1,
    rz0,
    rz1,
    rx2,
    rz2,
    gx,
    gz,
    cprev_x,
    cprev_z,
    cot,
    e2r,
    arb,
    sqb,
    squares,
    state,
    sca,
    s1r,
    s2r,
    s3b,
    s6r,
    lsem,
    psem,
    ssem,
    rsem,
):
    d = lax.axis_index("dp")
    t = lax.axis_index("tensor")
    c = lax.rem(t, 2)
    x = lax.rem(t // 2, 2)
    z = t // 4
    sib = (d, t + 1 - 2 * c)
    xn = (d, t + 2 - 4 * x)

    def zn(off):
        return (d, lax.rem(t + 4 * off, 16))

    def dpn(hop):
        return lax.rem(d // 4 + hop[0], 2) * 4 + lax.rem(d + hop[1], 4)

    def remote(src, dst, s, r, device):
        return pltpu.make_async_remote_copy(
            src_ref=src,
            dst_ref=dst,
            send_sem=ssem.at[s],
            recv_sem=rsem.at[r],
            device_id=device,
            device_id_type=MESH,
        )

    barrier = pltpu.get_barrier_semaphore()
    partners = [sib, xn] + [zn(o) for o in (1, 2, 3)] + [(dpn(hop), t) for hop in PEERS]
    for device in partners:
        pl.semaphore_signal(barrier, inc=1, device_id=device, device_id_type=MESH)

    def own_copy(j):
        columns = pl.ds(pl.multiple_of(c * CORE_WIDTH + j * PAIR, PAIR), PAIR)
        return pltpu.make_async_copy(
            w_ref.at[:, columns], wb.at[j, pl.ds(0, COLS)], lsem.at[j]
        )

    def other_copy(j):
        columns = pl.ds(pl.multiple_of((1 - c) * CORE_WIDTH + j * PAIR, PAIR), PAIR)
        return pltpu.make_async_copy(w_ref.at[:, columns], wtmp.at[j], lsem.at[CHUNKS + j])

    def w_copy(j):
        return remote(wsend.at[j], wrecv.at[j], S_W + j, R_W + j, sib)

    def order(i):
        return i // N_Z * N_Z + lax.rem(z + lax.rem(i + 2, N_Z), N_Z)

    def load(source, target, pieces, first):
        rows = source.shape[0] // pieces
        return [
            pltpu.make_async_copy(
                source.at[pl.ds(i * rows, rows)], target.at[pl.ds(i * rows, rows)], psem.at[first + i]
            )
            for i in range(pieces)
        ]

    load_inputs = load(inputs_ref, inputs_v, 4, 0)
    load_downs = [
        pltpu.make_async_copy(ref, down_v.at[pl.ds(i * RANK, RANK)], psem.at[4 + i])
        for i, ref in enumerate((dq_ref, dv_ref))
    ]
    half_rows = pl.ds(pl.multiple_of(x * HALF, HALF), HALF)

    def gap_lanes(s, region):
        left = c * CORE_WIDTH + (s * N_Z + z) * PAIR + region * LANES
        return pl.ds(pl.multiple_of(left, LANES), LANES)

    load_targets = []
    for s in range(STAGES):
        for i, (rows, target) in enumerate(((half_rows, targets_x), (pl.ds(0, ROWS), targets_z))):
            source = targets_ref.at[rows, gap_lanes(s, i)]
            load_targets.append(
                pltpu.make_async_copy(source, target.at[s], psem.at[6 + 2 * s + i])
            )

    def load_weights(i):
        rows = pl.ds(i * DEPTH, DEPTH)
        return [
            pltpu.make_async_copy(
                ref.at[rows],
                weights_v.at[rows, pl.ds(n * COLS, COLS)],
                psem.at[12 + 3 * i + n],
            )
            for n, ref in enumerate((wq_ref, wk_ref, wv_ref))
        ]

    pieces = [load_weights(i) for i in range(WIDTH // DEPTH)]
    for copy in load_inputs:
        copy.start()

    @pl.loop(0, CHUNKS)
    def _(i):
        other_copy(order(i)).start()

    for copy in load_downs + sum(pieces[:4], []):
        copy.start()

    for i, copy in enumerate(load_inputs):
        copy.wait()
        if i < 2:
            for late in pieces[4 + 2 * i] + pieces[5 + 2 * i]:
                late.start()
        if i == 2:

            @pl.loop(0, CHUNKS)
            def _(j):
                own_copy(order(j)).start()

            for late in load_targets:
                late.start()

        if i == 1:
            pl.semaphore_wait(barrier, len(partners))
        if i:

            @pl.loop(4 * (i - 1), 4 * i)
            def _(n):
                j = order(n)
                other_copy(j).wait()
                wsend[j] = wtmp[j].astype(F32)
                w_copy(j).start()

        size = ROWS // len(load_inputs)

        @pl.loop(i * size // 16, (i + 1) * size // 16)
        def _(r):
            rows = pl.ds(pl.multiple_of(r * 16, 16), 16)
            wide = inputs_v[rows, :].astype(F32)
            centred = wide - jnp.sum(wide, axis=1, keepdims=True) * (1.0 / WIDTH)
            spread = jnp.sum(centred * centred, axis=1, keepdims=True) * (1.0 / WIDTH)
            scaled = centred * lax.rsqrt(spread + EPS)
            normed[rows, :] = (scaled * gain_ref[...] + bias_ref[...]).astype(BF16)

    for i, piece in enumerate(pieces):
        for copy in piece:
            copy.wait()
        depth = pl.ds(i * DEPTH, DEPTH)
        product = dot(normed[:, depth], weights_v[depth, :])
        rows_v[...] = product if i == 0 else rows_v[...] + product
    for copy in load_downs:
        copy.wait()
    lows = dot_t(normed[...], down_v[...])
    lows_t = lows.T
    k_ref[...] = rows_v[:, COLS : 2 * COLS].astype(BF16)
    for i, (target, up) in enumerate(((q_ref, bq_ref), (v_ref, bv_ref))):
        ranks = slice(i * RANK, (i + 1) * RANK)
        high, rest = split_high_low(lows[:, ranks])
        u3[i] = jnp.concatenate([high, high, rest], axis=1)
        high, rest = split_high_low(lows_t[ranks])
        ut[i] = jnp.concatenate([high, rest], axis=0)
        high, rest = split_high_low(up[...])
        stacked = jnp.concatenate([high, rest, high], axis=0)
        rows = rows_v[:, 2 * i * COLS : (2 * i + 1) * COLS]
        target[...] = (rows + ADAPTER_SCALE * dot(u3[i], stacked)).astype(BF16)

    limit = len_ref[0]
    row = lax.broadcasted_iota(jnp.int32, (ROWS, ROWS), 0)
    col = lax.broadcasted_iota(jnp.int32, (ROWS, ROWS), 1)
    live = (col <= row) & (col < limit)
    lanes = [pl.ds(h * HEAD_DIM, HEAD_DIM) for h in range(HEADS)]
    scores = [dot_t(q_ref[:, n], k_ref[:, n]) * HEAD_DIM ** (-0.5) for n in lanes]
    scores = [jnp.where(live, a, NEG) for a in scores]
    weights = [jnp.exp(a - jnp.max(a, axis=-1, keepdims=True)) for a in scores]
    probs = [a / jnp.sum(a, axis=-1, keepdims=True) for a in weights]
    mixed = [dot(a.astype(BF16), v_ref[:, n]).astype(BF16) for a, n in zip(probs, lanes)]
    for h, n in enumerate(lanes):
        pf[h] = probs[h]
        pb[h] = probs[h].astype(BF16)
        pbt[h] = probs[h].T.astype(BF16)
        dmcat[:, n] = mixed[h]
        e1s[:, n] = mixed[h].astype(F32)
    place = lax.broadcasted_iota(jnp.int32, (ROWS, LANES), 0)
    mask_z = (place < limit).astype(F32)
    mask_x = (place[:HALF] + x * HALF < limit).astype(F32)
    for copy in load_targets:
        copy.wait()
    for s in range(STAGES):
        gap = inputs_v[half_rows, gap_lanes(s, 0)].astype(F32) - targets_x[s].astype(F32)
        cprev_x[s] = gap * mask_x
        gap = inputs_v[:, gap_lanes(s, 1)].astype(F32) - targets_z[s].astype(F32)
        cprev_z[s] = gap * mask_z
    state[...] = jnp.zeros_like(state)
    sca[...] = jnp.zeros_like(sca)

    @pl.loop(0, CG_STEPS + 1)
    def _(k):
        @pl.when(k > 0)
        def _():
            tangents = []
            for i in range(2):
                high, low = split_high_low(state[0, i * RANK : (i + 1) * RANK])
                stacked = jnp.concatenate([high, low, high], axis=0)
                tangents.append((ADAPTER_SCALE * dot(u3[i], stacked)).astype(BF16))
            dq, dv = [[a[:, h * HEAD_DIM : (h + 1) * HEAD_DIM] for h in range(HEADS)] for a in tangents]
            scores = [dot_t(a, k_ref[:, n]) * HEAD_DIM ** (-0.5) for a, n in zip(dq, lanes)]
            tilted = [pf[h] * a for h, a in enumerate(scores)]
            dprobs = [
                (a - pf[h] * jnp.sum(a, axis=-1, keepdims=True)).astype(BF16)
                for h, a in enumerate(tilted)
            ]
            left = [jnp.concatenate([a, pb[h]], axis=1) for h, a in enumerate(dprobs)]
            right = [jnp.concatenate([v_ref[:, n], a], axis=0) for a, n in zip(dv, lanes)]
            dmixed = [dot(a, b).astype(BF16) for a, b in zip(left, right)]
            for a, n in zip(dmixed, lanes):
                e1s[:, n] = a.astype(F32)
                dmcat[:, n] = a

        e1 = remote(e1s, e1r, S_E1, R_E1, sib)
        e1.start()
        sca[4] = jnp.broadcast_to(total(state[0] * state[0]), (8, 128))
        sca[5] = jnp.broadcast_to(total(state[0] * state[1]), (8, 128))
        s1 = remote(sca.at[pl.ds(4, 2)], s1r, S_S1, R_S1, sib)
        s1.start()
        @pl.when(k == 0)
        def _():
            for j in range(CHUNKS):
                own_copy(j).wait()

        for s in range(STAGES):
            for off in (2, 1, 3, 0):
                begun[s, off] = dot(dmcat[:, :PAIR], wb[s * N_Z + lax.rem(z + off, N_Z), :PAIR])
        e1.wait_recv()
        dmcat[:, pl.ds(COLS, COLS)] = e1r[...].astype(BF16)
        s1.wait_recv()
        sca[pl.ds(6, 2)] = sca[pl.ds(4, 2)] + s1r[...]
        s2 = remote(sca.at[pl.ds(6, 2)], s2r, S_S2, R_S2, xn)
        s2.start()

        def zi(off):
            return lax.rem(z + off, N_Z)

        def x1(s, off):
            i = N_Z * s + off
            source, target = part_x.at[s, 1 - x, zi(off)], rx1.at[s, zi(off)]
            return remote(source, target, S_X1 + i, R_X1 + i, xn)

        upper, lower = pl.ds(0, HALF), pl.ds(HALF, HALF)

        def z1(s, role):
            to, row, target = (
                (2, upper, rz0.at[s, 0]),
                (2, lower, rz0.at[s, 1]),
                (1, pl.ds(0, ROWS), rz1.at[s, 0]),
                (3, pl.ds(0, ROWS), rz1.at[s, 1]),
            )[role]
            i = 4 * s + role
            source = part_z.at[s, zi(to), row]
            return remote(source, target, S_Z1 + i, R_Z1 + i, zn(1 if role % 2 == 0 else 3))

        def x2(s, off):
            i = 3 * s + off - 1
            return remote(part_x.at[s, x, zi(off)], rx2.at[s, off - 1], S_X2 + i, R_X2 + i, zn(off))

        def z2(s):
            return remote(part_z.at[s, z], rz2.at[s], S_Z2 + s, R_Z2 + s, xn)

        for s in range(STAGES):

            @pl.when(k == 0)
            def _():
                for off in (2, 3, 0, 1):
                    j = s * N_Z + zi(off)
                    w_copy(j).wait_recv()
                    wb[j, pl.ds(COLS, COLS)] = wrecv[j].astype(BF16)

            for off in (2, 1, 3, 0):
                product = begun[s, off] + dot(dmcat[:, PAIR:], wb[s * N_Z + zi(off), PAIR:])
                part_z[s, zi(off)] = product[:, LANES:]
                for role in (0, 1) if off == 2 else ():
                    z1(s, role).start()
                part_x[s, 0, zi(off)] = product[:HALF, :LANES]
                part_x[s, 1, zi(off)] = product[HALF:, :LANES]
                x1(s, off).start()

        s2.wait_recv()
        s3b[z] = sca[pl.ds(6, 2)] + s2r[...]

        def s3(off, peer):
            return remote(s3b.at[peer], s3b.at[peer], S_S3 + off - 1, R_S3 + peer, zn(off))

        for off in (2, 1, 3):
            s3(off, z).start()

        for s in range(STAGES):
            z1(s, 0).wait_recv()
            part_z[s, zi(1), :HALF] = part_z[s, zi(1), :HALF] + rz0[s, 0]
            z1(s, 2).start()
            z1(s, 1).wait_recv()
            part_z[s, zi(3), HALF:] = part_z[s, zi(3), HALF:] + rz0[s, 1]
            z1(s, 3).start()

        def second_x(s):
            for off in (2, 1, 3, 0):
                x1(s, off).wait_recv()
                part_x[s, x, zi(off)] = part_x[s, x, zi(off)] + rx1[s, zi(off)]
                if off:
                    x2(s, off).start()

        def second_z(s):
            for role in (2, 3):
                z1(s, role).wait_recv()
            part_z[s, z] = part_z[s, z] + rz1[s, 0] + rz1[s, 1]
            z2(s).start()

        second_x(0)
        second_z(0)
        second_x(1)
        second_z(1)
        second_x(2)
        second_z(2)

        for off in (1, 2, 3):
            s3(off, zi(off)).wait_recv()
        sums = s3b[0] + s3b[1] + s3b[2] + s3b[3]
        sca[0] = sums[0]
        ratio = sums[0] / jnp.where(k > 1, sca[1], 1.0)
        beta = jnp.where(k == 0, 1.0, jnp.where(k == 1, 0.0, ratio))
        beta_row = beta[0:1, 0:1]
        sca[2] = sums[0] + 2.0 * beta * sums[1] + beta * beta * sca[2]

        def x3(s, off, peer):
            block = gx.at[s, x, peer]
            return remote(block, block, S_X3 + 3 * s + off - 1, R_X3 + N_Z * s + peer, zn(off))

        def x4(s, half, peer):
            block = gx.at[s, half, peer]
            i = N_Z * s + peer
            return remote(block, block, S_X4 + i, R_X4 + i, xn)

        def z4(s, role, incoming=False):
            if incoming:
                block = (
                    gz.at[s, zi(3)],
                    gz.at[s, zi(1)],
                    gz.at[s, zi(2), upper],
                    gz.at[s, zi(2), lower],
                )[role]
            else:
                block = (
                    gz.at[s, z],
                    gz.at[s, z],
                    gz.at[s, zi(3), upper],
                    gz.at[s, zi(1), lower],
                )[role]
            i = 4 * s + role
            return remote(block, block, S_Z4 + i, R_Z4 + i, zn(1 if role % 2 == 0 else 3))

        def own_x(s):
            for off in (1, 2, 3):
                x2(s, off).wait_recv()
            block = part_x[s, x, z] + rx2[s, 0] + rx2[s, 1] + rx2[s, 2]
            block = block * mask_x + beta_row * cprev_x[s]
            cprev_x[s] = block
            gx[s, x, z] = block
            for off in (2, 1, 3):
                x3(s, off, z).start()
            x4(s, x, z).start()

        def own_z(s):
            z2(s).wait_recv()
            block = part_z[s, z] + rz2[s]
            block = block * mask_z + beta_row * cprev_z[s]
            cprev_z[s] = block
            gz[s, z] = block
            z4(s, 0).start()
            z4(s, 1).start()

        def pass_x(s):
            for off in (1, 3, 2):
                x3(s, off, zi(off)).wait_recv()
                x4(s, x, zi(off)).start()

        def pass_z(s):
            for role in range(2):
                z4(s, role, True).wait_recv()
                z4(s, role + 2).start()

        own_x(0)
        own_x(1)
        own_z(0)
        own_x(2)
        own_z(1)
        own_z(2)
        pass_x(0)
        pass_x(1)
        pass_z(0)
        pass_x(2)
        pass_z(1)
        pass_z(2)
        state[1] = state[0] + beta_row * state[1]

        squares[...] = jnp.zeros_like(squares)
        for s in range(STAGES):
            for off in (0, 1, 3, 2):
                x4(s, 1 - x, zi(off)).wait_recv()
                if off == 2:
                    z4(s, 2, True).wait_recv()
                    z4(s, 3, True).wait_recv()
                left = jnp.concatenate([gx[s, 0, zi(off)], gx[s, 1, zi(off)]], axis=0)
                both = jnp.concatenate([left, gz[s, zi(off)]], axis=1)
                product = dot_t(both.astype(BF16), wb[s * N_Z + zi(off)])
                if s == 0 and off == 0:
                    cot[...] = product
                else:
                    cot[...] = cot[...] + product
                squares[...] = squares[...] + both * both

        e2 = remote(cot.at[:, pl.ds(COLS, COLS)], e2r, S_E2, R_E2, sib)
        e2.start()
        sca[3] = jnp.broadcast_to(total(squares[...]), (8, 128))
        s6 = remote(sca.at[3], s6r, S_S6, R_S6, sib)
        s6.start()
        s6.wait_recv()

        parity = lax.rem(k, 2)

        def ar(i, side, peer):
            block = arb.at[parity, peer, side]
            r = R_AR + (parity * N_DP + peer) * 2 + side
            return remote(block, block, S_AR + 2 * i + side, r, (dpn(PEERS[i]), t))

        def sq(i, peer):
            block = sqb.at[parity, peer]
            r = R_SQ + parity * N_DP + peer
            return remote(block, block, S_SQ + i, r, (dpn(PEERS[i]), t))

        sqb[parity, d] = sca[3] + s6r[...]
        for i in range(N_DP - 1):
            sq(i, d).start()
        e2.wait_recv()
        def gradient(side, cotangents):
            both = dot(ut[side], jnp.concatenate(cotangents, axis=1))
            arb[parity, d, side] = ADAPTER_SCALE * (both[:RANK] + both[RANK:])
            for i in range(N_DP - 1):
                ar(i, side, d).start()

        cotan = (cot[:, :COLS] + e2r[...]).astype(BF16)
        cotan = [cotan[:, h * HEAD_DIM : (h + 1) * HEAD_DIM] for h in range(HEADS)]
        gradient(1, [dot(pbt[h], a).astype(BF16) for h, a in enumerate(cotan)])
        dprobs = [dot_t(a, v_ref[:, n]) for a, n in zip(cotan, lanes)]
        tilted = [pf[h] * a for h, a in enumerate(dprobs)]
        dscores = [
            ((a - pf[h] * jnp.sum(a, axis=-1, keepdims=True)) * HEAD_DIM ** (-0.5)).astype(BF16)
            for h, a in enumerate(tilted)
        ]
        gradient(0, [dot(a, k_ref[:, n]).astype(BF16) for a, n in zip(dscores, lanes)])

        e1.wait_send()
        s1.wait_send()
        s2.wait_send()
        for off in (1, 2, 3):
            s3(off, z).wait_send()
        for s in range(STAGES):
            for off in range(N_Z):
                x1(s, off).wait_send()
            z2(s).wait_send()
            for off in (1, 2, 3):
                x2(s, off).wait_send()
                x3(s, off, z).wait_send()
            for peer in range(N_Z):
                x4(s, x, peer).wait_send()
                z4(s, peer).wait_send()
            for role in range(4):
                z1(s, role).wait_send()
        e2.wait_send()
        s6.wait_send()

        for i in reversed(range(N_DP - 1)):
            sq(i, dpn(PEERS[i])).wait_recv()
            for side in range(2):
                ar(i, side, dpn(PEERS[i])).wait_recv()
        for i in range(N_DP - 1):
            sq(i, d).wait_send()
            for side in range(2):
                ar(i, side, d).wait_send()
        summed = [arb[parity, 0, side] for side in range(2)]
        for peer in range(1, N_DP):
            summed = [a + arb[parity, peer, side] for side, a in enumerate(summed)]
        summed = jnp.concatenate(summed, axis=0)
        image = summed * (1.0 / (ROWS * N_DP)) + DAMP * state[1]
        squared = sqb[parity, 0]
        for peer in range(1, N_DP):
            squared = squared + sqb[parity, peer]
        squared = squared * (1.0 / (ROWS * N_DP))
        curvature = squared + DAMP * sca[2]
        alpha = jnp.where(k == 0, 1.0, sca[0] / jnp.where(k == 0, 1.0, curvature))[0:1, 0:1]
        state[2] = state[2] + jnp.where(k == 0, 0.0, alpha) * state[1]
        state[0] = state[0] - alpha * image
        sca[1] = sca[0]

    for j in range(CHUNKS):
        w_copy(j).wait_send()
    step_ref[...] = state[2]
    remain_ref[...] = state[0]


def solve(lengths, gain, bias, bq, bv, inputs, targets, wq, wk, wv, dq, dv, w_out):
    vmem = pl.BlockSpec(memory_space=pltpu.VMEM)
    square = (HEADS, HEAD_DIM, HEAD_DIM)
    half_block = (HALF, LANES)
    block = (ROWS, LANES)
    scratch = [
        pltpu.VMEM((ROWS, WIDTH), BF16),
        pltpu.VMEM((STAGES,) + half_block, BF16),
        pltpu.VMEM((STAGES,) + block, BF16),
        pltpu.VMEM((ROWS, WIDTH), BF16),
        pltpu.VMEM((WIDTH, 3 * COLS), BF16),
        pltpu.VMEM((ROWS, 3 * COLS), F32),
        pltpu.VMEM((2 * RANK, WIDTH), BF16),
        pltpu.VMEM((ROWS, COLS), BF16),
        pltpu.VMEM((ROWS, COLS), BF16),
        pltpu.VMEM((ROWS, COLS), BF16),
        pltpu.VMEM((CHUNKS, 2 * COLS, PAIR), BF16),
        pltpu.VMEM((CHUNKS, COLS, PAIR), BF16),
        pltpu.VMEM((CHUNKS, COLS, PAIR), F32),
        pltpu.VMEM((CHUNKS, COLS, PAIR), F32),
        pltpu.VMEM(square, F32),
        pltpu.VMEM(square, BF16),
        pltpu.VMEM(square, BF16),
        pltpu.VMEM((2, ROWS, 3 * RANK), BF16),
        pltpu.VMEM((2, 2 * RANK, ROWS), BF16),
        pltpu.VMEM((ROWS, 2 * COLS), BF16),
        pltpu.VMEM((STAGES, N_Z, ROWS, PAIR), F32),
        pltpu.VMEM((ROWS, COLS), F32),
        pltpu.VMEM((ROWS, COLS), F32),
        pltpu.VMEM((STAGES, 2, N_Z) + half_block, F32),
        pltpu.VMEM((STAGES, N_Z) + block, F32),
        pltpu.VMEM((STAGES, N_Z) + half_block, F32),
        pltpu.VMEM((STAGES, 2) + half_block, F32),
        pltpu.VMEM((STAGES, 2) + block, F32),
        pltpu.VMEM((STAGES, N_Z - 1) + half_block, F32),
        pltpu.VMEM((STAGES,) + block, F32),
        pltpu.VMEM((STAGES, 2, N_Z) + half_block, F32),
        pltpu.VMEM((STAGES, N_Z) + block, F32),
        pltpu.VMEM((STAGES,) + half_block, F32),
        pltpu.VMEM((STAGES,) + block, F32),
        pltpu.VMEM((ROWS, 2 * COLS), F32),
        pltpu.VMEM((ROWS, COLS), F32),
        pltpu.VMEM((2, N_DP, 2, RANK, COLS), F32),
        pltpu.VMEM((2, N_DP, 8, 128), F32),
        pltpu.VMEM((ROWS, PAIR), F32),
        pltpu.VMEM((3, 2 * RANK, COLS), F32),
        pltpu.VMEM((8, 8, 128), F32),
        pltpu.VMEM((2, 8, 128), F32),
        pltpu.VMEM((2, 8, 128), F32),
        pltpu.VMEM((N_Z, 2, 8, 128), F32),
        pltpu.VMEM((8, 128), F32),
        pltpu.SemaphoreType.DMA((2 * CHUNKS,)),
        pltpu.SemaphoreType.DMA((36,)),
        pltpu.SemaphoreType.DMA((N_SEND,)),
        pltpu.SemaphoreType.DMA((N_RECV,)),
    ]
    shape = jax.ShapeDtypeStruct((2 * RANK, COLS), F32)
    return pl.pallas_call(
        kernel,
        out_shape=(shape, shape),
        in_specs=[pl.BlockSpec(memory_space=pltpu.SMEM)]
        + [vmem] * 4
        + [pl.BlockSpec(memory_space=pl.ANY)] * 8,
        out_specs=(vmem, vmem),
        scratch_shapes=scratch,
        compiler_params=pltpu.CompilerParams(
            collective_id=0, has_side_effects=True, vmem_limit_bytes=58 * 2**20
        ),
        cost_estimate=pl.CostEstimate(
            flops=8 * 2 * ROWS * WIDTH * COLS, bytes_accessed=8 * 2**20, transcendentals=0
        ),
        name="newton",
    )(lengths, gain, bias, bq, bv, inputs, targets, wq, wk, wv, dq, dv, w_out)


def on_device(
    inputs,
    targets,
    lengths,
    ln_gain,
    ln_bias,
    query_weight,
    w_key,
    value_weight,
    w_out,
    down_query,
    down_value,
    query_up_factor,
    value_up_factor,
):
    step, remain = solve(
        lengths,
        ln_gain.reshape(1, WIDTH),
        ln_bias.reshape(1, WIDTH),
        query_up_factor,
        value_up_factor,
        inputs,
        targets,
        query_weight,
        w_key,
        value_weight,
        down_query.T,
        down_value.T,
        w_out,
    )
    return (step[:RANK], step[RANK:], remain[:RANK], remain[RANK:])


def solution(mesh):
    in_specs = (
        P("dp", None),
        P("dp", None),
        P("dp"),
        P(),
        P(),
        P(None, "tensor"),
        P(None, "tensor"),
        P(None, "tensor"),
        P("tensor", None),
        P(),
        P(),
        P(None, "tensor"),
        P(None, "tensor"),
    )
    out_specs = (P(None, "tensor"), P(None, "tensor"), P(None, "tensor"), P(None, "tensor"))
    return jax.shard_map(
        on_device, mesh=mesh, in_specs=in_specs, out_specs=out_specs, check_vma=False
    )
```
